32 devices in a mesh: dp: 2 (over y), ctx: 4 (over z), tp: 4 (over x, core).
Axes of the slice: x: 2, y: 2, z: 4, core: 2. Of those that a mesh axis runs over, the one named last changes fastest.
Arguments:
- hidden: bfloat16 [4, 2048, 1536], P('dp', 'ctx'), may hold values from -6 to 6
- cotangent: bfloat16 [4, 2048, 1536], P('dp', 'ctx'), may hold values from -6 to 6
- segments: int32 [4, 2048], P('dp', 'ctx'), may hold values from 0 to 2047, as said below
- valid: int32 [4, 2048], P('dp', 'ctx'), may hold values 0 or 1
- w_query: bfloat16 [1536, 1536], P(None, 'tp'), may hold values from -0.15625 to 0.15625
- w_key: bfloat16 [1536, 512], P(None, 'tp'), may hold values from -0.15625 to 0.15625
- w_value: bfloat16 [1536, 512], P(None, 'tp'), may hold values from -0.15625 to 0.15625
- w_out: bfloat16 [1536, 1536], P('tp'), may hold values from -1.5 to 1.5
- w_gate: bfloat16 [1536, 6912], P(None, 'tp'), may hold values from -0.15625 to 0.15625
- w_up: bfloat16 [1536, 6912], P(None, 'tp'), may hold values from -0.15625 to 0.15625
- w_down: bfloat16 [6912, 1536], P('tp'), may hold values from -0.078125 to 0.078125
- gain_attn: float32 [1536], replicated, may hold values from 0.4 to 1.6
- gain_ffn: float32 [1536], replicated, may hold values from 0.4 to 1.6
- gain_query: float32 [64], replicated, may hold values from 0.1 to 1.9
- gain_key: float32 [64], replicated, may hold values from 0.1 to 1.9
Outputs:
- output: bfloat16 [4, 2048, 1536], P('dp', 'ctx')
- grad_hidden: bfloat16 [4, 2048, 1536], P('dp', 'ctx')
- grad_query: float32 [1536, 1536], P(('dp', 'ctx'), 'tp')
- grad_key: float32 [1536, 512], P(('dp', 'ctx'), 'tp')
- grad_value: float32 [1536, 512], P(('dp', 'ctx'), 'tp')
- grad_out: float32 [1536, 1536], P('tp', ('dp', 'ctx'))
- grad_gate: float32 [1536, 6912], P(('dp', 'ctx'), 'tp')
- grad_up: float32 [1536, 6912], P(('dp', 'ctx'), 'tp')
- grad_down: float32 [6912, 1536], P('tp', ('dp', 'ctx'))
- grad_gain_attn: float32 [1536], replicated
- grad_gain_ffn: float32 [1536], replicated
- grad_gain_query: float32 [64], replicated
- grad_gain_key: float32 [64], replicated
- rms_hidden: float32 [], replicated
- rms_attn: float32 [], replicated
- rms_ffn: float32 [], replicated
The draws below stay inside these ranges and needn't reach their ends.
Inputs may be any that keep to these rules, and one draw needn't show every extreme that they name: `segments`: A token's number is the place in its sequence of its document's first token, so numbers never fall along a sequence; in every sequence one document begins within its first 512 tokens and ends within its last 512, and the last token is a document of its own.
All inputs are finite; a program needn't handle non-finite values. No bound on the sum of `valid` on one device may be relied on, other than what follows from the above.
Results may differ from the reference program's by a relative error of at most 0.017.
Values may be sent and summed in bfloat16 or wider, within the bound.
No kernel may reach another device: no remote copies, remote signals or barrier semaphores. Data moves between devices by JAX's collectives and lax.ppermute only.
A program may use at most 448 MiB of HBM per device.

```python
import jax
import jax.numpy as jnp
from jax import lax

D = 1536
HEADS = 24
KV_HEADS = 8
HEAD = 64
FF = 6912
LEN = 2048
LOCAL_LEN = 512
SEQS = 4


def draw_segments(key, part):
    key = jax.random.fold_in(key, 11)
    key_first, key_last, key_breaks = jax.random.split(key, 3)
    first = jax.random.randint(key_first, (SEQS, 1), 0, LOCAL_LEN)
    last = jax.random.randint(key_last, (SEQS, 1), LEN - LOCAL_LEN + 1, LEN + 1)
    places = jnp.arange(LEN)[None, :]
    breaks = (jax.random.randint(key_breaks, (SEQS, LEN), 0, 48) == 0).astype(jnp.int32)
    inside = (places > first) & (places < last)
    breaks = jnp.where(inside, 0, breaks)
    breaks = jnp.where((places == first) | (places == last) | (places == LEN - 1), 1, breaks)
    breaks = jnp.where(places == 0, 0, breaks)
    starts = jnp.where(breaks == 1, places, 0)
    return lax.cummax(starts, axis=1).astype(jnp.int32)


def set_ends(array, rng, low, top_value):
    place = [jax.random.randint(jax.random.fold_in(rng, axis), (), 0, length) for axis, length in enumerate(array.shape)]
    main_axis = array.shape.index(max(array.shape))
    neighbour = place[:main_axis] + [(place[main_axis] + 1) % array.shape[main_axis]] + place[main_axis + 1:]
    return array.at[tuple(place)].set(low).at[tuple(neighbour)].set(top_value)


def block_scale(stream_key, extent, cuts, smallest, high):
    loudness = 1.0
    for dim, parts in cuts:
        draws = jax.random.uniform(jax.random.fold_in(jax.random.fold_in(stream_key, 6), dim), (parts,), jnp.float32, smallest / len(cuts), high / len(cuts))
        loudness = loudness * jnp.repeat(jnp.exp(draws), extent[dim] // parts).reshape((-1,) + (1,) * (len(extent) - 1 - dim))
    return loudness


def noise(key, shape, spread, bound, cuts=(), kind=jnp.bfloat16):
    drawn = jax.random.normal(key, shape, jnp.float32) * spread
    if len(cuts) > 0:
        drawn = block_scale(key, shape, cuts, -0.22, 0.18) * drawn
    return jnp.clip(drawn, min=-bound, max=bound).astype(kind)


def setup_inputs(seed: int = 0) -> dict:
    streams_of = jax.random.split(jax.random.key(seed), 16)
    hidden = noise(streams_of[0], (SEQS, LEN, D), 1.0, 6.0, ((0, 2), (1, 4)))
    cotangent = noise(streams_of[1], (SEQS, LEN, D), 1.0, 6.0, ((0, 2), (1, 4)))
    segments = draw_segments(jax.random.fold_in(streams_of[15], 71), 0)
    valid = set_ends((jax.random.randint(streams_of[3], (SEQS, LEN), 0, 8) < 7).astype(jnp.int32), jax.random.fold_in(streams_of[3], 1), 0, 1)
    w_query = noise(streams_of[4], (D, HEADS * HEAD), D ** -0.5, 0.15625, ((1, 4),))
    w_key = noise(streams_of[5], (D, KV_HEADS * HEAD), D ** -0.5, 0.15625, ((1, 4),))
    w_value = noise(streams_of[6], (D, KV_HEADS * HEAD), D ** -0.5, 0.15625, ((1, 4),))
    w_out = noise(streams_of[7], (HEADS * HEAD, D), 16 ** -0.5, 1.5, ((0, 4),))
    w_gate = noise(streams_of[8], (D, FF), D ** -0.5, 0.15625, ((1, 4),))
    w_up = noise(streams_of[9], (D, FF), D ** -0.5, 0.15625, ((1, 4),))
    w_down = noise(streams_of[10], (FF, D), FF ** -0.5, 0.078125, ((0, 4),))
    gain_attn = jnp.clip(1.0 + 0.12 * jax.random.normal(streams_of[11], (D,), jnp.float32), 0.4, 1.6)
    gain_ffn = jnp.clip(1.0 + 0.12 * jax.random.normal(streams_of[12], (D,), jnp.float32), 0.4, 1.6)
    gain_query = jnp.clip(1.0 + 0.18 * jax.random.normal(streams_of[13], (HEAD,), jnp.float32), 0.1, 1.9)
    gain_key = jnp.clip(1.0 + 0.18 * jax.random.normal(streams_of[14], (HEAD,), jnp.float32), 0.1, 1.9)
    return dict(hidden=hidden, cotangent=cotangent, segments=segments, valid=valid, w_query=w_query, w_key=w_key, w_value=w_value, w_out=w_out, w_gate=w_gate, w_up=w_up, w_down=w_down, gain_attn=gain_attn, gain_ffn=gain_ffn, gain_query=gain_query, gain_key=gain_key)


EPS = 1e-05
THETA = 1000000.0

@jax.custom_vjp
def low(v):
    return lax.optimization_barrier(v.astype(jnp.bfloat16)).astype(jnp.float32)

@jax.custom_vjp
def low_back(v):
    return v

def low_keep(v):
    return (low(v), None)

def low_pass(kept, grad):
    return (grad,)

def back_keep(v):
    return (v, None)

def back_low(kept, grad):
    return (low(grad),)
low.defvjp(low_keep, low_pass)
low_back.defvjp(back_keep, back_low)

def rms_scale(values):
    return lax.rsqrt(lax.optimization_barrier(jnp.mean(values * values, axis=-1, keepdims=True)) + EPS)

def rope_tables(length):
    places = jnp.arange(length).astype(jnp.float32)
    freqs = THETA ** (-jnp.arange(HEAD // 2).astype(jnp.float32) / (HEAD // 2))
    angles = places[:, None] * freqs[None, :]
    return (jnp.cos(angles), jnp.sin(angles))

def rotate(values, cosines, sines):
    half = values.shape[-1] // 2
    first = values[..., :half]
    second = values[..., half:]
    cos_b = cosines[:, None, :]
    sin_b = sines[:, None, :]
    return jnp.concatenate([first * cos_b - second * sin_b, second * cos_b + first * sin_b], axis=-1)

def both(values):
    return low(low_back(values))

def attend(query, keys, values, docs):
    length = query.shape[0]
    block = min(512, length)
    count = length // block
    group = HEADS // KV_HEADS
    key_places = jnp.arange(length)
    highest = lax.Precision.HIGHEST

    def one_block(item):
        query_block, query_places, query_docs = item
        grouped = query_block.reshape(block, KV_HEADS, group, HEAD)
        scores = jnp.einsum('bgrd,kgd->grbk', grouped, keys, precision=highest) * 0.125
        scores = low_back(scores)
        allowed = (query_places[:, None] >= key_places[None, :]) & (query_docs[:, None] == docs[None, :])
        scores = jnp.where(allowed[None, None], scores, -1e+30)
        largest = lax.optimization_barrier(jnp.max(scores, axis=-1, keepdims=True))
        weights = jnp.exp(scores - largest)
        probs = weights / lax.optimization_barrier(jnp.sum(weights, axis=-1, keepdims=True))
        mixed = jnp.einsum('grbk,kgd->bgrd', low(probs), values, precision=highest)
        return mixed.reshape(block, HEADS * HEAD)
    items = (query.reshape(count, block, HEADS, HEAD), key_places.reshape(count, block), docs.reshape(count, block))
    return lax.map(jax.checkpoint(one_block), items).reshape(length, HEADS * HEAD)

def layer(hidden, docs, w_query, w_key, w_value, w_out, w_gate, w_up, w_down, gain_attn, gain_ffn, gain_query, gain_key):
    highest = lax.Precision.HIGHEST
    length = hidden.shape[0]
    normed = low(hidden * rms_scale(hidden) * gain_attn)
    query = low_back(jnp.dot(normed, w_query, precision=highest)).reshape(length, HEADS, HEAD)
    keys = low_back(jnp.dot(normed, w_key, precision=highest)).reshape(length, KV_HEADS, HEAD)
    values = both(jnp.dot(normed, w_value, precision=highest)).reshape(length, KV_HEADS, HEAD)
    cosines, sines = rope_tables(length)
    query = both(rotate(query * rms_scale(query) * gain_query, cosines, sines))
    keys = both(rotate(keys * rms_scale(keys) * gain_key, cosines, sines))
    mixed = both(attend(query, keys, values, docs))
    attn = low_back(jnp.dot(mixed, w_out, precision=highest))
    middle = hidden + attn
    normed_two = low(middle * rms_scale(middle) * gain_ffn)
    gate = low_back(jnp.dot(normed_two, w_gate, precision=highest))
    upper = low_back(jnp.dot(normed_two, w_up, precision=highest))
    active = low(gate * jax.nn.sigmoid(gate) * upper)
    branch = jnp.dot(active, w_down, precision=highest)
    return (middle + branch, (attn, branch))

def reference(hidden, cotangent, segments, valid, w_query, w_key, w_value, w_out, w_gate, w_up, w_down, gain_attn, gain_ffn, gain_query, gain_key):
    hidden_f = hidden.astype(jnp.float32)
    weights_f = tuple((weight.astype(jnp.float32) for weight in (w_query, w_key, w_value, w_out, w_gate, w_up, w_down, gain_attn, gain_ffn, gain_query, gain_key)))

    def forward(hidden_all, *weight_list):

        def step(carry, item):
            rows_in, docs = item
            result, extra = jax.checkpoint(layer)(rows_in, docs, *weight_list)
            return (carry, (result, extra))
        carry_out, (outputs, extras) = lax.scan(step, jnp.zeros((), jnp.float32), (hidden_all, segments))
        return (outputs, extras)
    outputs, pullback, extras = jax.vjp(forward, hidden_f, *weights_f, has_aux=True)
    grads = pullback(cotangent.astype(jnp.float32))
    attn_all, branch_all = extras
    mask = valid.astype(jnp.float32)
    count = jnp.maximum(jnp.sum(mask), 1.0)

    def rms_of(field):
        return jnp.sqrt(jnp.sum(mask[..., None] * field * field) / (count * D))
    return (outputs.astype(jnp.bfloat16), grads[0].astype(jnp.bfloat16), grads[1], grads[2], grads[3], grads[4], grads[5], grads[6], grads[7], grads[8], grads[9], grads[10], grads[11], rms_of(hidden_f), rms_of(attn_all), rms_of(branch_all))
```

```python
import functools

import jax
import jax.numpy as jnp
import numpy as np
from jax import lax
from jax.experimental import pallas as pl
from jax.experimental.pallas import tpu as pltpu
from jax.sharding import PartitionSpec as P

HEAD = 64
EPS = 1e-05
THETA = 1000000.0
BF = jnp.bfloat16
F32 = jnp.float32
LANES = 128
VMEM_LIMIT = 56 * 1024 * 1024


def nn_dot(left, right):
    return lax.dot_general(left, right, (((1,), (0,)), ((), ())), preferred_element_type=F32)


def nt_dot(left, right):
    return lax.dot_general(left, right, (((1,), (1,)), ((), ())), preferred_element_type=F32)


def tn_dot(left, right):
    return lax.dot_general(left, right, (((0,), (0,)), ((), ())), preferred_element_type=F32)


def rms_scale(values):
    return lax.rsqrt(jnp.mean(values * values, axis=-1, keepdims=True) + EPS)


def norm_back(grads, unit, scale, gain):
    scaled = grads * gain
    return scale * (scaled - unit * jnp.mean(scaled * unit, axis=-1, keepdims=True))


def lane_of(shape):
    return lax.broadcasted_iota(jnp.int32, shape, len(shape) - 1)


def head_mean(slab):
    row = lax.broadcasted_iota(jnp.int32, (LANES, LANES), 0)
    col = lax.broadcasted_iota(jnp.int32, (LANES, LANES), 1)
    same = jnp.where((row < HEAD) == (col < HEAD), 1.0 / HEAD, 0.0).astype(F32)
    return lax.dot_general(
        slab,
        same,
        (((1,), (0,)), ((), ())),
        precision=lax.Precision.HIGHEST,
        preferred_element_type=F32,
    )


def turn(slab, cosines, sines):
    half = HEAD // 2
    lane = lane_of(slab.shape)
    partner = jnp.where(
        (lane & (HEAD - 1)) < half,
        pltpu.roll(slab, LANES - half, 1),
        pltpu.roll(slab, half, 1),
    )
    return slab * cosines + partner * sines


def with_ones(slab, which):
    wide = slab.astype(F32)
    if which == 1:
        wide = pltpu.roll(wide, HEAD, 1)
    lane = lane_of(wide.shape)
    return jnp.where(lane < HEAD, wide, jnp.where(lane < HEAD + 3, 1.0, 0.0))


def with_minus(low, column):
    first = (-column).astype(BF).astype(F32)
    rest = -column - first
    second = rest.astype(BF).astype(F32)
    third = rest - second
    lane = lane_of(low.shape)
    tail = jnp.where(
        lane == HEAD,
        first,
        jnp.where(lane == HEAD + 1, second, jnp.where(lane == HEAD + 2, third, 0.0)),
    )
    return jnp.where(lane < HEAD, low, tail).astype(BF)


def low_head(ref, head):
    slab = ref[:, (head // 2) * LANES : (head // 2 + 1) * LANES].astype(F32)
    return pltpu.roll(slab, HEAD, 1) if head % 2 else slab


def project_kernel(
    hidden, gain, wq, wk, wv, cosines, sines, gain_q, gain_k, normed, query, kv, q_raw, k_raw
):
    x = hidden[...].astype(F32)
    unit = x * rms_scale(x)
    rows = (unit * gain[...]).astype(BF)
    normed[...] = rows
    cos_v = cosines[...]
    sin_v = sines[...]

    def place(raw, gains):
        return turn(raw * lax.rsqrt(head_mean(raw * raw) + EPS) * gains, cos_v, sin_v)

    key = nn_dot(rows, wk[...])
    k_raw[...] = key
    kv[:, :LANES] = place(key, gain_k[...]).astype(BF)
    kv[:, LANES:] = nn_dot(rows, wv[...]).astype(BF)
    raw = nn_dot(rows, wq[...])
    q_raw[...] = raw
    for slab in range(raw.shape[1] // LANES):
        at = slice(slab * LANES, (slab + 1) * LANES)
        query[:, at] = (place(raw[:, at], gain_q[...]).astype(BF).astype(F32) * 0.125).astype(BF)


def attend_kernel(tile, info, seg, query, *refs):
    pieces = refs[:-5]
    mixed, ext, low, total, _ = refs[-5:]
    rows = query.shape[0]
    heads = query.shape[1] // HEAD
    group = heads // 2
    me = info[0]
    first_doc = info[1]
    lane = lane_of((rows, LANES))
    for head in range(heads):
        low[head] = jnp.where(lane < HEAD, low_head(query, head), 0.0).astype(BF)
    total[...] = jnp.zeros_like(total)

    def tile_step(back, block, piece):
        start = (me - back) * rows + block * tile

        @pl.when(start + tile > first_doc)
        def _():
            kv = piece[pl.ds(block * tile, tile), :]
            shape = (rows, tile)
            place = start + lax.broadcasted_iota(jnp.int32, shape, 1)
            allowed = place >= seg[...]
            if back == 0:
                allowed &= place <= me * rows + lax.broadcasted_iota(jnp.int32, shape, 0)
            for which in range(2):
                key = with_ones(kv[:, :LANES], which).astype(BF)
                value = with_ones(kv[:, LANES:], which).astype(BF)
                for head in range(which * group, (which + 1) * group):
                    scores = jnp.where(allowed, nt_dot(low[head], key), -1e30)
                    total[head] += nn_dot(jnp.exp(scores).astype(BF), value)

    for back, piece in enumerate(pieces):

        @pl.when(me >= back)
        def _(back=back, piece=piece):
            def step(block, carry):
                tile_step(back, block, piece)
                return carry

            lax.fori_loop(0, rows // tile, step, 0)

    for slab in range(heads // 2):
        parts = []
        for head in (2 * slab, 2 * slab + 1):
            got = total[head]
            weight = got[:, HEAD : HEAD + 1]
            parts.append(got / weight)
            ext[head] = with_minus(low[head].astype(F32), jnp.log(weight))
        joined = jnp.where(lane < HEAD, parts[0], pltpu.roll(parts[1], HEAD, 1))
        mixed[:, slab * LANES : (slab + 1) * LANES] = joined.astype(BF)


def attend_back_kernel(
    tile, count, info, seg, ext, mixed, d_mixed, q_raw, cosines, sines, gain_q, *refs
):
    pieces = refs[:count]
    d_q_raw, gain_part = refs[count : count + 2]
    d_pieces = refs[count + 2 : 2 * count + 2]
    d_ext, d_query = refs[2 * count + 2 :]
    rows = mixed.shape[0]
    heads = mixed.shape[1] // HEAD
    group = heads // 2
    me = info[0]
    first_doc = info[1]
    lane = lane_of((rows, LANES))
    for head in range(heads):
        grad = jnp.where(lane < HEAD, low_head(d_mixed, head), 0.0)
        delta = jnp.sum(grad * low_head(mixed, head), axis=-1, keepdims=True)
        d_ext[head] = with_minus(grad, delta)
    d_query[...] = jnp.zeros_like(d_query)
    low_tile = lane_of((tile, LANES)) < HEAD

    def tile_step(back, block, piece, d_piece):
        start = (me - back) * rows + block * tile
        needed = start + tile > first_doc
        at = pl.ds(block * tile, tile)

        @pl.when(needed)
        def _():
            kv = piece[at, :]
            shape = (tile, rows)
            place = start + lax.broadcasted_iota(jnp.int32, shape, 0)
            allowed = place >= seg[...]
            if back == 0:
                allowed &= place <= me * rows + lax.broadcasted_iota(jnp.int32, shape, 1)
            d_keys = []
            d_values = []
            for which in range(2):
                key_f = with_ones(kv[:, :LANES], which)
                key = key_f.astype(BF)
                key_t = key_f.T[:HEAD].astype(BF)
                value = with_ones(kv[:, LANES:], which).astype(BF)
                d_key = jnp.zeros((tile, LANES), F32)
                d_value = jnp.zeros((tile, LANES), F32)
                for head in range(which * group, (which + 1) * group):
                    scores = jnp.where(allowed, nt_dot(key, ext[head]), -1e30)
                    probs = jnp.exp(scores)
                    d_scores = (probs * nt_dot(value, d_ext[head])).astype(BF)
                    d_value += nn_dot(probs.astype(BF), d_ext[head])
                    d_key += nn_dot(d_scores, ext[head])
                    d_query[head * HEAD : (head + 1) * HEAD, :] += nn_dot(key_t, d_scores)
                d_keys.append(d_key)
                d_values.append(d_value)
            for spot, pair in enumerate((d_keys, d_values)):
                joined = jnp.where(low_tile, pair[0], pltpu.roll(pair[1], HEAD, 1))
                d_piece[at, spot * LANES : (spot + 1) * LANES] = joined.astype(BF)

        @pl.when(jnp.logical_not(needed))
        def _():
            d_piece[at, :] = jnp.zeros((tile, 2 * LANES), BF)

    for back, (piece, d_piece) in enumerate(zip(pieces, d_pieces)):

        @pl.when(me >= back)
        def _(back=back, piece=piece, d_piece=d_piece):
            def step(block, carry):
                tile_step(back, block, piece, d_piece)
                return carry

            lax.fori_loop(0, rows // tile, step, 0)

        @pl.when(me < back)
        def _(d_piece=d_piece):
            d_piece[...] = jnp.zeros_like(d_piece)

    for slab in range(heads // 2):
        at = slice(slab * LANES, (slab + 1) * LANES)
        grad = (d_query[at, :].T * 0.125).astype(BF).astype(F32)
        out, part = rope_norm_back(grad, q_raw[:, at], cosines[...], sines[...], gain_q[...])
        d_q_raw[:, at] = out
        gain_part[:, at] = part


def rope_norm_back(grad, raw, cosines, sines, gains):
    back = turn(grad, cosines, -sines)
    scale = lax.rsqrt(head_mean(raw * raw) + EPS)
    unit = raw * scale
    scaled = back * gains
    out = scale * (scaled - unit * head_mean(scaled * unit))
    part = jnp.sum(back * unit, axis=0, keepdims=True)
    return out.astype(BF), part


def key_back_kernel(grad, k_raw, cosines, sines, gain_k, d_kv, gain_part):
    d_key = grad[:, :LANES].astype(BF).astype(F32)
    out, part = rope_norm_back(d_key, k_raw[...], cosines[...], sines[...], gain_k[...])
    d_kv[:, :LANES] = out
    d_kv[:, LANES:] = grad[:, LANES:].astype(BF)
    gain_part[...] = part


def rope_tables(length):
    places = np.arange(length).astype(np.float32)
    half = HEAD // 2
    freqs = np.float32(THETA) ** (-np.arange(half).astype(np.float32) / np.float32(half))
    angles = (places[:, None] * freqs.astype(np.float32)[None, :]).astype(np.float64)
    cosines = np.cos(angles).astype(np.float32)
    sines = np.sin(angles).astype(np.float32)
    return (
        np.concatenate([cosines] * 4, axis=1),
        np.concatenate([-sines, sines, -sines, sines], axis=1),
    )


def build(mesh):
    dp_n, ctx_n, tp_n = (mesh.shape[a] for a in ("dp", "ctx", "tp"))
    flip = lambda n, bit: [(i, i ^ bit) for i in range(n)]
    up = [(i, i + 1) for i in range(ctx_n - 1)]
    down = [(i + 1, i) for i in range(ctx_n - 1)]

    def params():
        return pltpu.CompilerParams(vmem_limit_bytes=VMEM_LIMIT)

    def cut(array, start, size):
        return lax.dynamic_slice_in_dim(array, start, size, axis=0)

    def spread(part):
        me = lax.axis_index("tp")
        half = part.shape[0] // 2
        low = me % 2
        got = lax.ppermute(cut(part, (1 - low) * half, half), "tp", flip(tp_n, 1))
        both = cut(part, low * half, half).astype(F32) + got.astype(F32)
        high = me // 2
        quarter = half // 2
        got = lax.ppermute(cut(both, (1 - high) * quarter, quarter).astype(BF), "tp", flip(tp_n, 2))
        return cut(both, high * quarter, quarter) + got.astype(F32)

    def own_start(rows):
        me = lax.axis_index("tp")
        return (me % 2) * (rows // 2) + (me // 2) * (rows // 4)

    def join(mine, other, first):
        return jnp.where(
            first, jnp.concatenate([mine, other]), jnp.concatenate([other, mine])
        )

    def collect(own):
        me = lax.axis_index("tp")
        half = join(own, lax.ppermute(own, "tp", flip(tp_n, 2)), me // 2 == 0)
        return join(half, lax.ppermute(half, "tp", flip(tp_n, 1)), me % 2 == 0)

    def sum_all(values):
        for axis, size in (("tp", tp_n), ("ctx", ctx_n), ("dp", dp_n)):
            bit = 1
            while bit < size:
                values = values + lax.ppermute(values, axis, flip(size, bit))
                bit *= 2
        return values

    def scatter_sum(left, right):
        width = left.shape[1]
        mine = lax.axis_index("dp")
        if dp_n == 2:
            half = width // 2
            take = lambda which: lax.dynamic_slice_in_dim(left, which * half, half, axis=1)
            away = tn_dot(take(1 - mine), right).astype(BF)
            got = lax.ppermute(away, "dp", flip(2, 1))
            part = tn_dot(take(mine), right) + got.astype(F32)
        else:
            part = lax.psum_scatter(
                tn_dot(left, right).astype(BF), "dp", scatter_dimension=0, tiled=True
            ).astype(F32)
        me = lax.axis_index("ctx")
        block = part.shape[0] // ctx_n
        pick = lambda which: cut(part, jnp.clip(which, 0, ctx_n - 1) * block, block)
        rise = fall = jnp.zeros((), F32)
        for step in range(1, ctx_n):
            send_up = (pick(me + ctx_n - step) + rise).astype(BF)
            send_down = (pick(me - ctx_n + step) + fall).astype(BF)
            rise = lax.ppermute(send_up, "ctx", up[:step]).astype(F32)
            fall = lax.ppermute(send_down, "ctx", down[ctx_n - 1 - step :]).astype(F32)
        return pick(me) + rise + fall

    def body(
        hidden,
        cotangent,
        segments,
        valid,
        w_query,
        w_key,
        w_value,
        w_out,
        w_gate,
        w_up,
        w_down,
        gain_attn,
        gain_ffn,
        gain_query,
        gain_key,
    ):
        seqs, local, width = hidden.shape
        rows = seqs * local
        q_cols = w_query.shape[1]
        heads = q_cols // HEAD
        me = lax.axis_index("ctx")
        cos_np, sin_np = rope_tables(local * ctx_n)
        cosines = cut(jnp.asarray(cos_np), me * local, local)
        sines = cut(jnp.asarray(sin_np), me * local, local)
        hidden_r = hidden.reshape(rows, width)
        cot = cotangent.reshape(rows, width)
        gq = jnp.concatenate([gain_query, gain_query])[None]
        gk = jnp.concatenate([gain_key, gain_key])[None]

        step_rows = 256
        per = local // step_rows
        by_row = lambda cols: pl.BlockSpec((step_rows, cols), lambda i: (i, 0))
        whole = lambda r, c: pl.BlockSpec((r, c), lambda i: (0, 0))
        table = pl.BlockSpec((step_rows, LANES), lambda i: (i % per, 0))
        normed, query, kv, q_raw, k_raw = pl.pallas_call(
            project_kernel,
            grid=(rows // step_rows,),
            in_specs=[
                by_row(width),
                whole(1, width),
                whole(width, q_cols),
                whole(width, LANES),
                whole(width, LANES),
                table,
                table,
                whole(1, LANES),
                whole(1, LANES),
            ],
            out_specs=[
                by_row(width),
                by_row(q_cols),
                by_row(2 * LANES),
                by_row(q_cols),
                by_row(LANES),
            ],
            out_shape=[
                jax.ShapeDtypeStruct((rows, width), BF),
                jax.ShapeDtypeStruct((rows, q_cols), BF),
                jax.ShapeDtypeStruct((rows, 2 * LANES), BF),
                jax.ShapeDtypeStruct((rows, q_cols), F32),
                jax.ShapeDtypeStruct((rows, LANES), F32),
            ],
            compiler_params=params(),
            name="project",
        )(
            hidden_r,
            gain_attn[None],
            w_query,
            w_key,
            w_value,
            cosines,
            sines,
            gq,
            gk,
        )

        tile = 256
        smem = pl.BlockSpec(memory_space=pltpu.SMEM)
        pieces = []
        infos = []
        fulls = lambda r, c: pl.BlockSpec((r, c), lambda i: (0, 0))
        for seq in range(seqs):
            piece = [kv[seq * local : (seq + 1) * local]]
            for _ in range(ctx_n - 1):
                piece.append(lax.ppermute(piece[-1], "ctx", up))
            pieces.append(piece)
            infos.append(jnp.stack([me, segments[seq, 0]]).astype(jnp.int32))

        mixed = []
        exts = []
        attn = []
        for seq in range(seqs):
            at_seq = lambda c, seq=seq: pl.BlockSpec((local, c), lambda i: (seq, 0))
            mix, ext = pl.pallas_call(
                functools.partial(attend_kernel, tile),
                grid=(1,),
                in_specs=[smem, fulls(local, 1), at_seq(q_cols)] + [fulls(local, 2 * LANES)] * ctx_n,
                out_specs=[
                    fulls(local, q_cols),
                    pl.BlockSpec((heads, local, LANES), lambda i: (0, 0, 0)),
                ],
                out_shape=[
                    jax.ShapeDtypeStruct((local, q_cols), BF),
                    jax.ShapeDtypeStruct((heads, local, LANES), BF),
                ],
                scratch_shapes=[
                    pltpu.VMEM((heads, local, LANES), BF),
                    pltpu.VMEM((heads, local, LANES), F32),
                    pltpu.VMEM((8, LANES), F32),
                ],
                compiler_params=params(),
                name="attend",
            )(infos[seq], segments[seq][:, None], query, *pieces[seq])
            mixed.append(mix)
            exts.append(ext)
            attn.append(spread(nn_dot(mix, w_out).astype(BF)))

        start = own_start(local)
        quarter = local // tp_n
        take = lambda array: jnp.concatenate(
            [cut(array[s * local : (s + 1) * local], start, quarter) for s in range(seqs)]
        )
        hidden_own = take(hidden_r).astype(F32)
        cot_own = take(cot).astype(F32)
        valid_own = take(valid.reshape(rows)).astype(F32)
        attn_own = jnp.concatenate(attn)
        middle = hidden_own + attn_own
        scale_two = rms_scale(middle)
        unit_two = middle * scale_two
        normed_own = (unit_two * gain_ffn).astype(BF)
        regather = lambda own: jnp.concatenate(
            [collect(own[s * quarter : (s + 1) * quarter]) for s in range(seqs)]
        )
        normed_two = regather(normed_own)

        d_active = nt_dot(cot, w_down)
        gate = nn_dot(normed_two, w_gate)
        upper = nn_dot(normed_two, w_up)
        sigma = jax.nn.sigmoid(gate)
        active = (gate * sigma * upper).astype(BF)
        d_upper = (d_active * gate * sigma).astype(BF)
        d_gate = (d_active * upper * sigma * (1.0 + gate * (1.0 - sigma))).astype(BF)

        branch_part = nn_dot(active, w_down).astype(BF)
        d_two_part = (nt_dot(d_gate, w_gate) + nt_dot(d_upper, w_up)).astype(BF)
        by_seq = lambda array: [array[s * local : (s + 1) * local] for s in range(seqs)]
        d_two = jnp.concatenate([spread(p) for p in by_seq(d_two_part)])
        branch = jnp.concatenate([spread(p) for p in by_seq(branch_part)])
        output = regather((middle + branch).astype(BF)).reshape(seqs, local, width)

        grad_down = scatter_sum(cot, active).T
        grad_gate = scatter_sum(normed_two, d_gate)
        grad_up = scatter_sum(normed_two, d_upper)

        gain_ffn_part = jnp.sum(d_two * unit_two, axis=0)
        d_middle = cot_own + norm_back(d_two, unit_two, scale_two, gain_ffn)
        d_middle_b = regather(d_middle.astype(BF))
        grad_out = scatter_sum(d_middle_b, jnp.concatenate(mixed)).T
        d_mixed = nt_dot(d_middle_b, w_out).astype(BF)

        d_q_raw = []
        d_kv_raw = []
        gain_q_part = jnp.zeros((1, HEAD), F32)
        gain_k_part = jnp.zeros((1, HEAD), F32)
        for seq in range(seqs):
            at_seq = lambda c, seq=seq: pl.BlockSpec((local, c), lambda i: (seq, 0))
            outs = pl.pallas_call(
                functools.partial(attend_back_kernel, tile, ctx_n),
                grid=(1,),
                in_specs=[
                    smem,
                    fulls(1, local),
                    pl.BlockSpec((heads, local, LANES), lambda i: (0, 0, 0)),
                    fulls(local, q_cols),
                    at_seq(q_cols),
                    at_seq(q_cols),
                    fulls(local, LANES),
                    fulls(local, LANES),
                    fulls(1, LANES),
                ]
                + [fulls(local, 2 * LANES)] * ctx_n,
                out_specs=[fulls(local, q_cols), fulls(1, q_cols)]
                + [fulls(local, 2 * LANES)] * ctx_n,
                out_shape=[
                    jax.ShapeDtypeStruct((local, q_cols), BF),
                    jax.ShapeDtypeStruct((1, q_cols), F32),
                ]
                + [jax.ShapeDtypeStruct((local, 2 * LANES), BF)] * ctx_n,
                scratch_shapes=[
                    pltpu.VMEM((heads, local, LANES), BF),
                    pltpu.VMEM((q_cols, local), F32),
                ],
                compiler_params=params(),
                name="attend_back",
            )(
                infos[seq],
                segments[seq][None],
                exts[seq],
                mixed[seq],
                d_mixed,
                q_raw,
                cosines,
                sines,
                gq,
                *pieces[seq],
            )
            d_q_raw.append(outs[0])
            gain_q_part += jnp.sum(outs[1].reshape(heads, HEAD), axis=0, keepdims=True)
            d_pieces = outs[2:]
            passed = d_pieces[ctx_n - 1]
            for back in range(ctx_n - 1, 0, -1):
                got = lax.ppermute(passed, "ctx", down)
                passed = d_pieces[back - 1].astype(F32) + got.astype(F32)
                if back > 1:
                    passed = passed.astype(BF)
            d_kv, part = pl.pallas_call(
                key_back_kernel,
                grid=(1,),
                in_specs=[
                    fulls(local, 2 * LANES),
                    at_seq(LANES),
                    fulls(local, LANES),
                    fulls(local, LANES),
                    fulls(1, LANES),
                ],
                out_specs=[fulls(local, 2 * LANES), fulls(1, LANES)],
                out_shape=[
                    jax.ShapeDtypeStruct((local, 2 * LANES), BF),
                    jax.ShapeDtypeStruct((1, LANES), F32),
                ],
                compiler_params=params(),
                name="key_back",
            )(passed, k_raw, cosines, sines, gk)
            d_kv_raw.append(d_kv)
            gain_k_part += part[:, :HEAD] + part[:, HEAD:]

        w_kv = jnp.concatenate([w_key, w_value], axis=1)
        d_one = []
        for seq in range(seqs):
            part = nt_dot(d_q_raw[seq], w_query) + nt_dot(d_kv_raw[seq], w_kv)
            d_one.append(spread(part.astype(BF)))
        d_one = jnp.concatenate(d_one)
        scale_one = rms_scale(hidden_own)
        unit_one = hidden_own * scale_one
        gain_attn_part = jnp.sum(d_one * unit_one, axis=0)
        grad_own = (d_middle + norm_back(d_one, unit_one, scale_one, gain_attn)).astype(BF)
        grad_hidden = regather(grad_own).reshape(seqs, local, width)
        d_qkv = jnp.concatenate(
            [jnp.concatenate(d_q_raw), jnp.concatenate(d_kv_raw)], axis=1
        )
        grad_qkv = scatter_sum(normed, d_qkv)
        grad_query = grad_qkv[:, :q_cols]
        grad_key = grad_qkv[:, q_cols : q_cols + LANES]
        grad_value = grad_qkv[:, q_cols + LANES :]

        square = lambda values: jnp.sum(valid_own * jnp.sum(values * values, axis=-1))
        small = jnp.concatenate(
            [
                gain_attn_part,
                gain_ffn_part,
                gain_q_part[0],
                gain_k_part[0],
                jnp.stack(
                    [square(hidden_own), square(attn_own), square(branch), jnp.sum(valid_own)]
                ),
                jnp.zeros((LANES - 4,), F32),
            ]
        )
        small = sum_all(small.reshape(-1, LANES)).reshape(-1)
        at = 2 * width + 2 * HEAD
        denom = jnp.maximum(small[at + 3], 1.0) * width
        root = lambda spot: jnp.sqrt(small[at + spot] / denom)
        return (
            output,
            grad_hidden,
            grad_query,
            grad_key,
            grad_value,
            grad_out,
            grad_gate,
            grad_up,
            grad_down,
            small[:width],
            small[width : 2 * width],
            small[2 * width : 2 * width + HEAD],
            small[2 * width + HEAD : at],
            root(0),
            root(1),
            root(2),
        )

    return body


def solution(mesh):
    tokens = P("dp", "ctx", None)
    marks = P("dp", "ctx")
    columns = P(None, "tp")
    rows = P("tp", None)
    by_rows = P(("dp", "ctx"), "tp")
    by_columns = P("tp", ("dp", "ctx"))
    in_specs = (tokens, tokens, marks, marks, columns, columns, columns, rows)
    in_specs += (columns, columns, rows, P(), P(), P(), P())
    out_specs = (tokens, tokens, by_rows, by_rows, by_rows, by_columns, by_rows, by_rows)
    out_specs += (by_columns, P(), P(), P(), P(), P(), P(), P())
    return jax.shard_map(
        build(mesh), mesh=mesh, in_specs=in_specs, out_specs=out_specs, check_vma=False
    )
```

```python
import functools

import jax
import jax.numpy as jnp
import numpy as np
from jax import lax
from jax.experimental import pallas as pl
from jax.experimental.pallas import tpu as pltpu
from jax.sharding import PartitionSpec as P

HEAD = 64
EPS = 1e-05
THETA = 1000000.0
BF = jnp.bfloat16
F32 = jnp.float32
LANES = 128
VMEM_LIMIT = 56 * 1024 * 1024


def nn_dot(left, right):
    return lax.dot_general(left, right, (((1,), (0,)), ((), ())), preferred_element_type=F32)


def nt_dot(left, right):
    return lax.dot_general(left, right, (((1,), (1,)), ((), ())), preferred_element_type=F32)


def tn_dot(left, right):
    return lax.dot_general(left, right, (((0,), (0,)), ((), ())), preferred_element_type=F32)


def rms_scale(values):
    return lax.rsqrt(jnp.mean(values * values, axis=-1, keepdims=True) + EPS)


def norm_back(grads, unit, scale, gain):
    scaled = grads * gain
    return scale * (scaled - unit * jnp.mean(scaled * unit, axis=-1, keepdims=True))


def lane_of(shape):
    return lax.broadcasted_iota(jnp.int32, shape, len(shape) - 1)


def head_mean(slab):
    row = lax.broadcasted_iota(jnp.int32, (LANES, LANES), 0)
    col = lax.broadcasted_iota(jnp.int32, (LANES, LANES), 1)
    same = jnp.where((row < HEAD) == (col < HEAD), 1.0 / HEAD, 0.0).astype(BF)
    high = slab.astype(BF)
    rest = slab - high.astype(F32)
    mid = rest.astype(BF)
    low = (rest - mid.astype(F32)).astype(BF)
    return nn_dot(high, same) + nn_dot(mid, same) + nn_dot(low, same)


def turn(slab, cosines, sines):
    half = HEAD // 2
    lane = lane_of(slab.shape)
    partner = jnp.where(
        (lane & (HEAD - 1)) < half,
        pltpu.roll(slab, LANES - half, 1),
        pltpu.roll(slab, half, 1),
    )
    return slab * cosines + partner * sines


def with_ones(slab, which):
    wide = slab.astype(F32)
    if which == 1:
        wide = pltpu.roll(wide, HEAD, 1)
    lane = lane_of(wide.shape)
    return jnp.where(lane < HEAD, wide, jnp.where(lane < HEAD + 3, 1.0, 0.0))


def with_minus(low, column):
    first = (-column).astype(BF).astype(F32)
    rest = -column - first
    second = rest.astype(BF).astype(F32)
    third = rest - second
    lane = lane_of(low.shape)
    tail = jnp.where(
        lane == HEAD,
        first,
        jnp.where(lane == HEAD + 1, second, jnp.where(lane == HEAD + 2, third, 0.0)),
    )
    return jnp.where(lane < HEAD, low, tail).astype(BF)


def low_head(ref, head):
    slab = ref[:, (head // 2) * LANES : (head // 2 + 1) * LANES].astype(F32)
    return pltpu.roll(slab, HEAD, 1) if head % 2 else slab


def project_kernel(
    spots, hidden, gain, wq, wk, wv, cosines, sines, gain_q, gain_k, normed, query, kv, q_raw, k_raw
):
    x = hidden[...].astype(F32)
    unit = x * rms_scale(x)
    rows = (unit * gain[...]).astype(BF)
    normed[...] = rows
    cos_v = cosines[...]
    sin_v = sines[...]

    def place(raw, gains):
        return turn(raw * lax.rsqrt(head_mean(raw * raw) + EPS) * gains, cos_v, sin_v)

    key = nn_dot(rows, wk[...])
    k_raw[...] = key
    kv[:, :LANES] = place(key, gain_k[...]).astype(BF)
    kv[:, LANES:] = nn_dot(rows, wv[...]).astype(BF)
    raw = nn_dot(rows, wq[...])
    q_raw[...] = raw
    for slab in range(raw.shape[1] // LANES):
        at = slice(slab * LANES, (slab + 1) * LANES)
        query[:, at] = (place(raw[:, at], gain_q[...]).astype(BF).astype(F32) * 0.125).astype(BF)


def attend_kernel(tile, seq, spots, seg_row, query, w_out, *refs):
    pieces = refs[:-10]
    moved, *sums = refs[-10:-5]
    mixed, ext, low, total, seg = refs[-5:]
    rows = query.shape[0]
    heads = query.shape[1] // HEAD
    group = heads // 2
    me = spots[4]
    first_doc = spots[5 + seq]
    wide_row = jnp.broadcast_to(seg_row[...].astype(F32), (LANES, rows))
    seg[...] = wide_row.T[:, :1].astype(jnp.int32)
    lane = lane_of((rows, LANES))
    for head in range(heads):
        low[head] = jnp.where(lane < HEAD, low_head(query, head), 0.0).astype(BF)
    total[...] = jnp.zeros_like(total)

    def tile_step(back, block, piece):
        start = (me - back) * rows + block * tile

        @pl.when(start + tile > first_doc)
        def _():
            kv = piece[pl.ds(block * tile, tile), :]
            shape = (rows, tile)
            place = start + lax.broadcasted_iota(jnp.int32, shape, 1)
            allowed = place >= seg[...]
            if back == 0:
                allowed &= place <= me * rows + lax.broadcasted_iota(jnp.int32, shape, 0)
            for which in range(2):
                key = with_ones(kv[:, :LANES], which).astype(BF)
                value = with_ones(kv[:, LANES:], which).astype(BF)
                for head in range(which * group, (which + 1) * group):
                    scores = jnp.where(allowed, nt_dot(low[head], key), -1e30)
                    total[head] += nn_dot(jnp.exp(scores).astype(BF), value)

    for back, piece in enumerate(pieces):

        @pl.when(me >= back)
        def _(back=back, piece=piece):
            def step(block, carry):
                tile_step(back, block, piece)
                return carry

            lax.fori_loop(0, rows // tile, step, 0)

    for slab in range(heads // 2):
        parts = []
        for head in (2 * slab, 2 * slab + 1):
            got = total[head]
            weight = got[:, HEAD : HEAD + 1]
            parts.append(got / weight)
            ext[head] = with_minus(low[head].astype(F32), jnp.log(weight))
        joined = jnp.where(lane < HEAD, parts[0], pltpu.roll(parts[1], HEAD, 1))
        mixed[:, slab * LANES : (slab + 1) * LANES] = joined.astype(BF)
    block = rows // 4
    for i, at in enumerate(spots_of(spots, 4, rows)):
        moved[i * block : (i + 1) * block, :] = mixed[at, :]
    split_rows(nn_dot(moved[...], w_out[...]), *sums)


def attend_back_kernel(
    tile,
    count,
    seq,
    spots,
    seg,
    ext,
    mixed,
    own,
    near,
    far,
    far_near,
    w_out,
    q_raw,
    cosines,
    sines,
    gain_q,
    *refs,
):
    pieces = refs[:count]
    d_rows, d_q_raw, gain_part = refs[count : count + 3]
    d_pieces = refs[count + 3 : 2 * count + 3]
    d_ext, d_query, d_mixed = refs[2 * count + 3 :]
    rows = mixed.shape[0]
    heads = mixed.shape[1] // HEAD
    group = heads // 2
    me = spots[4]
    first_doc = spots[5 + seq]
    lane = lane_of((rows, LANES))
    block = rows // 4
    for i, part in enumerate((own, near, far, far_near)):
        d_rows[i * block : (i + 1) * block, :] = part[...]
    moved = nt_dot(d_rows[...], w_out[...]).astype(BF)
    for i, at in enumerate(spots_of(spots, 4, rows)):
        d_mixed[at, :] = moved[i * block : (i + 1) * block]
    for head in range(heads):
        grad = jnp.where(lane < HEAD, low_head(d_mixed, head), 0.0)
        delta = jnp.sum(grad * low_head(mixed, head), axis=-1, keepdims=True)
        d_ext[head] = with_minus(grad, delta)
    d_query[...] = jnp.zeros_like(d_query)
    low_tile = lane_of((tile, LANES)) < HEAD

    def tile_step(back, block, piece, d_piece):
        start = (me - back) * rows + block * tile
        needed = start + tile > first_doc
        at = pl.ds(block * tile, tile)

        @pl.when(needed)
        def _():
            kv = piece[at, :]
            shape = (tile, rows)
            place = start + lax.broadcasted_iota(jnp.int32, shape, 0)
            allowed = place >= seg[...]
            if back == 0:
                allowed &= place <= me * rows + lax.broadcasted_iota(jnp.int32, shape, 1)
            d_keys = []
            d_values = []
            for which in range(2):
                key_f = with_ones(kv[:, :LANES], which)
                key = key_f.astype(BF)
                key_t = key_f.T[:HEAD].astype(BF)
                value = with_ones(kv[:, LANES:], which).astype(BF)
                d_key = jnp.zeros((tile, LANES), F32)
                d_value = jnp.zeros((tile, LANES), F32)
                for head in range(which * group, (which + 1) * group):
                    scores = jnp.where(allowed, nt_dot(key, ext[head]), -1e30)
                    probs = jnp.exp(scores)
                    d_scores = (probs * nt_dot(value, d_ext[head])).astype(BF)
                    d_value += nn_dot(probs.astype(BF), d_ext[head])
                    d_key += nn_dot(d_scores, ext[head])
                    d_query[head * HEAD : (head + 1) * HEAD, :] += nn_dot(key_t, d_scores)
                d_keys.append(d_key)
                d_values.append(d_value)
            for spot, pair in enumerate((d_keys, d_values)):
                joined = jnp.where(low_tile, pair[0], pltpu.roll(pair[1], HEAD, 1))
                d_piece[at, spot * LANES : (spot + 1) * LANES] = joined.astype(BF)

        @pl.when(jnp.logical_not(needed))
        def _():
            d_piece[at, :] = jnp.zeros((tile, 2 * LANES), BF)

    for back, (piece, d_piece) in enumerate(zip(pieces, d_pieces)):

        @pl.when(me >= back)
        def _(back=back, piece=piece, d_piece=d_piece):
            def step(block, carry):
                tile_step(back, block, piece, d_piece)
                return carry

            lax.fori_loop(0, rows // tile, step, 0)

        @pl.when(me < back)
        def _(d_piece=d_piece):
            d_piece[...] = jnp.zeros_like(d_piece)

    for slab in range(heads // 2):
        at = slice(slab * LANES, (slab + 1) * LANES)
        grad = (d_query[at, :].T * 0.125).astype(BF).astype(F32)
        out, part = rope_norm_back(grad, q_raw[:, at], cosines[...], sines[...], gain_q[...])
        d_q_raw[:, at] = out
        gain_part[:, at] = part


def rope_norm_back(grad, raw, cosines, sines, gains):
    back = turn(grad, cosines, -sines)
    scale = lax.rsqrt(head_mean(raw * raw) + EPS)
    unit = raw * scale
    scaled = back * gains
    out = scale * (scaled - unit * head_mean(scaled * unit))
    part = jnp.sum(back * unit, axis=0, keepdims=True)
    return out.astype(BF), part


def key_back_kernel(
    quarters,
    d_piece,
    got,
    d_q_raw,
    k_raw,
    cosines,
    sines,
    gain_k,
    w_query,
    w_key,
    w_value,
    d_qkv,
    own,
    near,
    far,
    far_near,
    gain_part,
    moved,
):
    q_cols = d_q_raw.shape[1]
    total = (d_piece[...].astype(F32) + got[...].astype(F32)).astype(BF)
    d_key = total[:, :LANES].astype(F32)
    out, part = rope_norm_back(d_key, k_raw[...], cosines[...], sines[...], gain_k[...])
    gain_part[...] = part
    d_qkv[:, :q_cols] = d_q_raw[...]
    d_qkv[:, q_cols : q_cols + LANES] = out
    d_qkv[:, q_cols + LANES :] = total[:, LANES:]
    block = moved.shape[0] // 4
    for i, at in enumerate(spots_of(quarters, 4, moved.shape[0])):
        moved[i * block : (i + 1) * block, :] = d_qkv[at, :]
    grad = nt_dot(moved[:, :q_cols], w_query[...])
    grad += nt_dot(moved[:, q_cols : q_cols + LANES], w_key[...])
    grad += nt_dot(moved[:, q_cols + LANES :], w_value[...])
    split_rows(grad, own, near, far, far_near)


def spots_of(spots, count, rows, skip=0):
    block = rows // count
    return [pl.ds(pl.multiple_of(spots[skip + i] * block, 16), block) for i in range(count)]


def split_rows(total, *parts):
    block = total.shape[0] // len(parts)
    for i, part in enumerate(parts):
        part[...] = total[i * block : (i + 1) * block].astype(part.dtype)


def d_active_kernel(quarters, rows, right, moved, out):
    @pl.when(pl.program_id(0) == 0)
    def _():
        block = rows.shape[0] // 4
        for i, at in enumerate(spots_of(quarters, 4, rows.shape[0])):
            moved[i * block : (i + 1) * block, :] = rows[at, :]

    out[...] = nt_dot(moved[...], right[...]).astype(BF)


def units_kernel(
    units, own, near, far, far_near, gate_t, up_t, d_active, rows, active, d_gate, d_upper
):
    @pl.when(pl.program_id(0) == 0)
    def _():
        block = own.shape[0]
        for i, part in enumerate((own, near, far, far_near)):
            rows[i * block : (i + 1) * block, :] = part[...]

    x = rows[...]
    wide = active.shape[1]
    half = wide // 2
    for part in range(2):
        at = slice(part * half, (part + 1) * half)
        gate = nt_dot(x, gate_t[at, :])
        upper = nt_dot(x, up_t[at, :])
        column = pl.program_id(0) * wide + part * half + lane_of(gate.shape)
        real = column < units
        sigma = jax.nn.sigmoid(gate)
        silu = gate * sigma
        grad = d_active[:, at].astype(F32)
        active[:, at] = jnp.where(real, silu * upper, 0.0).astype(BF)
        d_upper[:, at] = jnp.where(real, grad * silu, 0.0).astype(BF)
        slope = grad * upper * (sigma + silu * (1.0 - sigma))
        d_gate[:, at] = jnp.where(real, slope, 0.0).astype(BF)


def columns_kernel(count, *refs):
    depth = refs[count].shape[0]
    total = sum(nn_dot(refs[i][:, :depth], refs[count + i][...]) for i in range(count))
    split_rows(total, *refs[2 * count :])


def masked_sum(valid, values):
    mask = jnp.broadcast_to(valid[0].astype(F32), (8, values.shape[0]))
    total = lax.dot_general(
        mask,
        values,
        (((1,), (0,)), ((), ())),
        precision=lax.Precision.HIGHEST,
        preferred_element_type=F32,
    )
    return total[:1]


def pass_back_kernel(first, second, *refs):
    out = refs[-1]
    local = first.shape[0]
    for i, part in enumerate((first, second)):
        at = slice(i * local, (i + 1) * local)
        if len(refs) > 1:
            out[at, :] = (part[...].astype(F32) + refs[0][at, :].astype(F32)).astype(BF)
        else:
            out[at, :] = part[...]


def norm_two_kernel(spot, kept, got_far, got, hidden, valid, gain, normed, middle, squares):
    attn = kept[...] + got_far[...].astype(F32) + got[...].astype(F32)
    before = hidden[...].astype(F32)
    total = before + attn
    middle[...] = total
    normed[...] = (total * rms_scale(total) * gain[...]).astype(BF)
    squares[0:1, :] = masked_sum(valid, attn * attn)
    squares[1:2, :] = masked_sum(valid, before * before)


def middle_back_kernel(spot, kept, got_far, got, middle, cot, gain, d_low, d_middle, gain_part):
    grad = kept[...] + got_far[...].astype(F32) + got[...].astype(F32)
    before = middle[...]
    scale = rms_scale(before)
    unit = before * scale
    gain_part[...] = jnp.sum(grad * unit, axis=0, keepdims=True)
    total = cot[...].astype(F32) + norm_back(grad, unit, scale, gain[...])
    d_middle[...] = total
    d_low[...] = total.astype(BF)


def hidden_back_kernel(spot, kept, got_far, got, hidden, d_middle, gain, out, gain_part):
    grad = kept[...] + got_far[...].astype(F32) + got[...].astype(F32)
    before = hidden[...].astype(F32)
    scale = rms_scale(before)
    unit = before * scale
    gain_part[...] = jnp.sum(grad * unit, axis=0, keepdims=True)
    out[...] = (d_middle[...] + norm_back(grad, unit, scale, gain[...])).astype(BF)


def output_kernel(spot, kept, got_far, got, middle, valid, out, squares):
    branch = kept[...] + got_far[...].astype(F32) + got[...].astype(F32)
    out[...] = (middle[...] + branch).astype(BF)
    squares[...] = masked_sum(valid, branch * branch)


def place_kernel(quarters, *refs):
    parts, out = refs[:-1], refs[-1]
    block = parts[0].shape[0]
    for i, part in enumerate(parts):
        first = pl.multiple_of((i // 4 * 4 + quarters[i % 4]) * block, 16)
        out[pl.ds(first, block), :] = part[...]


def rope_tables(length):
    places = np.arange(length).astype(np.float32)
    half = HEAD // 2
    freqs = np.float32(THETA) ** (-np.arange(half).astype(np.float32) / np.float32(half))
    angles = (places[:, None] * freqs.astype(np.float32)[None, :]).astype(np.float64)
    cosines = np.cos(angles).astype(np.float32)
    sines = np.sin(angles).astype(np.float32)
    return (
        np.concatenate([cosines] * 4, axis=1),
        np.concatenate([-sines, sines, -sines, sines], axis=1),
    )


def after(value, *others):
    return lax.optimization_barrier((value,) + others)[0]


def params():
    return pltpu.CompilerParams(vmem_limit_bytes=VMEM_LIMIT)


def call(kernel, name, **kw):
    small = pl.CostEstimate(flops=1, bytes_accessed=1, transcendentals=0)
    return pl.pallas_call(kernel, compiler_params=params(), cost_estimate=small, name=name, **kw)


def shape(*dims, dtype=BF):
    return jax.ShapeDtypeStruct(dims, dtype)


def fixed(*dims):
    return pl.BlockSpec(dims, lambda i: (0,) * len(dims))


def by_row(rows, cols, first=0):
    return pl.BlockSpec((rows, cols), lambda i: (first + i, 0))


def by_block(rows, cols, spot):
    return pl.BlockSpec((rows, cols), lambda i: (spot, 0))


def by_col(rows, cols):
    return pl.BlockSpec((rows, cols), lambda i: (0, i))


SMEM = pl.BlockSpec(memory_space=pltpu.SMEM)
UNITS = 512
PAD = 256


def flip(n, bit):
    return [(i, i ^ bit) for i in range(n)]


def cut(array, start, size):
    return lax.dynamic_slice_in_dim(array, start, size, axis=0)


class Order:
    def __init__(self):
        self.last = None

    def tie(self, *values):
        if self.last is not None:
            values = lax.optimization_barrier(values + (self.last,))[:-1]
        return values

    def mark(self, value):
        self.last = value
        return value

    def wait(self, values, spot):
        values[spot] = self.mark(self.tie(values[spot])[0])


def build(mesh):
    dp_n, ctx_n, tp_n = (mesh.shape[a] for a in ("dp", "ctx", "tp"))
    blocks = dp_n * ctx_n

    def bits(axis, n):
        out = []
        while n > 1:
            n //= 2
            out.append((axis, n))
        return out

    steps = bits("dp", dp_n) + bits("ctx", ctx_n)[::-1]
    sizes = {"dp": dp_n, "ctx": ctx_n, "tp": tp_n}

    def swap(value, step):
        axis, bit = step
        return lax.ppermute(value, axis, flip(sizes[axis], bit))

    core, across = ("tp", 1), ("tp", 2)

    def bit_of(step):
        axis, bit = step
        return lax.axis_index(axis) // bit % 2

    def halves(part, step):
        axis, bit = step
        if axis == "dp":
            view = part.reshape(1, 2, -1, part.shape[-1])
        else:
            left = ctx_n // (2 * bit)
            view = part.reshape(left, 2, -1, part.shape[-1])
        mine = bit_of(step)
        pick = lambda which: lax.dynamic_index_in_dim(view, which, 1, keepdims=False).reshape(
            -1, part.shape[-1]
        )
        return pick(mine), pick(1 - mine)

    def body(
        hidden,
        cotangent,
        segments,
        valid,
        w_query,
        w_key,
        w_value,
        w_out,
        w_gate,
        w_up,
        w_down,
        gain_attn,
        gain_ffn,
        gain_query,
        gain_key,
    ):
        seqs, local, width = hidden.shape
        rows = seqs * local
        every = range(seqs)
        q_cols = w_query.shape[1]
        units = w_gate.shape[1]
        wide = pl.cdiv(units, PAD) * PAD
        heads = q_cols // HEAD
        me = lax.axis_index("ctx")
        member = lax.axis_index("tp")
        o = Order()
        cosines, sines = (jnp.asarray(t) for t in rope_tables(local * ctx_n))
        hidden_r = hidden.reshape(rows, width)
        cot_r = cotangent.reshape(rows, width)
        valid_r = valid.reshape(seqs * 4, 1, local // 4)
        gate_t, up_t = w_gate.T, w_up.T
        gq = jnp.concatenate([gain_query, gain_query])[None]
        gk = jnp.concatenate([gain_key, gain_key])[None]
        gain_a, gain_f = gain_attn[None], gain_ffn[None]
        tile = 256
        half, quarter = local // 2, local // 4
        own = (member % 2) * 2 + member // 2
        spots = jnp.stack([own ^ i for i in range(4)] + [me])
        spots = jnp.concatenate([spots, segments[:, 0]]).astype(jnp.int32)
        seg_rows = [segments[s][None] for s in every]
        _, *seg_rows = lax.optimization_barrier((spots, *seg_rows))

        def stage(kernel, name, args, outs, grid=1, scratch=(), placed=False, shared=None):
            arrays = [a for a, _ in args]
            arrays[:1] = o.tie(arrays[0])
            fix = lambda spec: pl.BlockSpec(spec.block_shape, lambda i, *s: spec.index_map(i))
            of = lambda spec: spec.spec if isinstance(spec, Dynamic) else fix(spec)
            specs = [of(spec) for _, spec in args]
            old = list(shared or [])
            count = int(placed) + len(args)
            run = kernel
            if old:
                run = lambda *refs: kernel(*refs[:count], *refs[count + len(old) :])
            got = pl.pallas_call(
                run,
                grid_spec=pltpu.PrefetchScalarGridSpec(
                    num_scalar_prefetch=int(placed),
                    grid=(grid,),
                    in_specs=specs + [pl.BlockSpec(memory_space=pl.ANY)] * len(old),
                    out_specs=[fix(s) for _, s in outs],
                    scratch_shapes=list(scratch),
                ),
                out_shape=[s for s, _ in outs],
                input_output_aliases={count + i: i for i in range(len(old))},
                compiler_params=params(),
                cost_estimate=pl.CostEstimate(flops=1, bytes_accessed=1, transcendentals=0),
                name=name,
            )(*([spots] if placed else []), *arrays, *old)
            o.mark(got[0])
            return got

        class Dynamic:
            def __init__(self, cols, seq):
                self.spec = pl.BlockSpec((quarter, cols), lambda i, s: (seq * 4 + s[0], 0))

        def full(array):
            return (array, fixed(*array.shape))

        def fulls(arrays):
            return [full(a) for a in arrays]

        def new(*dims, dtype=BF):
            return (shape(*dims, dtype=dtype), fixed(*dims))

        def part(cols, s):
            return by_block(local, cols, s)

        class Table(Dynamic):
            def __init__(self, rows):
                per = local // rows
                self.spec = pl.BlockSpec((rows, LANES), lambda i, s: (s[4] * per + i, 0))

        class Valid(Dynamic):
            def __init__(self, seq):
                self.spec = pl.BlockSpec((1, 1, quarter), lambda i, s: (seq * 4 + s[0], 0, 0))

        tables = lambda n: [(t, Table(n)) for t in (cosines, sines)]

        parts_out = [
            (shape(quarter, width, dtype=d), fixed(quarter, width)) for d in (F32, F32, BF, BF)
        ]

        def split_columns(s, lefts, rights, name):
            count = len(lefts)
            depth, cols = rights[0].shape
            return stage(
                functools.partial(columns_kernel, count),
                name,
                [(l, part(l.shape[1], s)) for l in lefts] + [(r, by_col(depth, UNITS)) for r in rights],
                [(out, by_col(quarter, UNITS)) for out, _ in parts_out],
                grid=cols // UNITS,
            )

        class Spread:
            def __init__(self, own, near, far, far_near):
                self.own, self.near = own, near
                self.far = [far_near, far]

            def first(self):
                self.far = list(o.tie(*self.far))
                o.mark(self.far[0])
                self.got = [swap(f, core) for f in self.far]

            def second(self):
                near, got = o.tie(self.near, self.got[0])
                away = o.mark((near + got.astype(F32)).astype(BF))
                self.got[0] = swap(away, across)

            def parts(self):
                return fulls([self.own, self.got[1], self.got[0]])

        class Collect:
            def __init__(self, mine):
                self.got = [mine, swap(mine, across)]

            def second(self):
                o.wait(self.got, 1)
                self.got += [swap(value, core) for value in self.got]

        class Grad:
            def __init__(self, *pairs):
                self.pairs = pairs
                self.half = width // 2

            def product(self, which, rights):
                parts = []
                for (left, _), right in zip(self.pairs, rights):
                    rows = lax.dynamic_slice_in_dim(left, which * self.half, self.half, axis=1)
                    parts.append(tn_dot(rows, right))
                return parts

            def away(self):
                rights = o.tie(*[right for _, right in self.pairs])
                parts = self.product(1 - bit_of(steps[0]), rights)
                self.out = o.mark(jnp.concatenate([p.astype(BF) for p in parts], axis=1))

            def send(self, *waits):
                for grad in waits:
                    grad.wait()
                (out,) = o.tie(self.out)
                self.got = swap(o.mark(out), steps[0])

            def wait(self):
                (self.got,) = o.tie(self.got)
                o.mark(self.got)

            def own(self):
                *rights, got = o.tie(*[right for _, right in self.pairs], self.got)
                parts = self.product(bit_of(steps[0]), rights)
                ends = np.cumsum([p.shape[1] for p in parts])
                total = jnp.concatenate(
                    [p + got[:, e - p.shape[1] : e].astype(F32) for p, e in zip(parts, ends)],
                    axis=1,
                )
                self.left_steps = steps[1:]
                self.terms = [o.mark(total)]
                self.pass_on()

            def pass_on(self):
                if not self.left_steps:
                    return
                step = self.left_steps.pop(0)
                pairs = [halves(t, step) for t in self.terms]
                away = sum(p[1].astype(F32) for p in pairs).astype(BF)
                self.terms = [p[0] for p in pairs] + [swap(o.mark(away), step)]

            def third(self):
                (self.terms[-1],) = o.tie(self.terms[-1])
                self.pass_on()

            def last(self):
                while self.left_steps:
                    self.third()
                (self.terms[-1],) = o.tie(self.terms[-1])
                return o.mark(sum(t.astype(F32) for t in self.terms))

        up = lambda hops: [(i, i + hops) for i in range(ctx_n - hops)]
        down = [(i + 1, i) for i in range(ctx_n - 1)]
        normed, query, q_raw, k_raw = None, [], [], []
        pieces = []
        step = 256
        for s in every:
            outs = stage(
                project_kernel,
                "project",
                [(hidden_r, by_row(step, width, s * (local // step)))]
                + fulls([gain_a, w_query, w_key, w_value])
                + tables(step)
                + fulls([gq, gk]),
                [(shape(rows, width), by_row(step, width, s * (local // step)))]
                + [
                    (shape(local, c, dtype=d), by_row(step, c))
                    for c, d in (
                        (q_cols, BF),
                        (2 * LANES, BF),
                        (q_cols, F32),
                        (LANES, F32),
                    )
                ],
                grid=local // step,
                placed=True,
                shared=[normed] if s else None,
            )
            normed = outs[0]
            for into, value in zip((query, pieces, q_raw, k_raw), outs[1:]):
                into.append([value] if into is pieces else value)
            for hops in range(1, min(3, ctx_n)):
                pieces[s].append(lax.ppermute(outs[2], "ctx", up(hops)))

        d_active, cot_moved = [], None

        def d_active_of(s):
            nonlocal cot_moved
            cot_moved, grad = stage(
                d_active_kernel,
                "d_active",
                [(cot_r, part(width, s)), (w_down, by_row(UNITS, width))],
                [
                    (shape(rows, width), part(width, s)),
                    (shape(local, wide), by_col(local, UNITS)),
                ],
                grid=pl.cdiv(wide, UNITS),
                placed=True,
                shared=[cot_moved] if s else None,
            )
            d_active.append(grad)

        d_active_of(0)
        for spot in range(1, len(pieces[0])):
            o.wait(pieces[0], spot)
        for _ in range(3, ctx_n):
            pieces[0].append(lax.ppermute(pieces[0][-1], "ctx", up(1)))
        for s in every[1:]:
            d_active_of(s)
            for spot in range(1, len(pieces[s])):
                o.wait(pieces[s], spot)
            for _ in range(3, ctx_n):
                pieces[s].append(lax.ppermute(pieces[s][-1], "ctx", up(1)))

        mixed, mixed_moved, exts, attn = [], None, [], []

        def attend(s):
            nonlocal mixed_moved
            mixed_moved, *parts, mix, ext = stage(
                functools.partial(attend_kernel, tile, s),
                "attend",
                fulls([seg_rows[s], query[s], w_out] + pieces[s]),
                [(shape(rows, q_cols), part(q_cols, s))]
                + parts_out
                + [new(local, q_cols), new(heads, local, LANES)],
                scratch=[
                    pltpu.VMEM((heads, local, LANES), BF),
                    pltpu.VMEM((heads, local, LANES), F32),
                    pltpu.VMEM((local, 1), jnp.int32),
                ],
                placed=True,
                shared=[mixed_moved] if s else None,
            )
            mixed.append(mix)
            exts.append(ext)
            attn.append(Spread(*parts))

        middle, squares, two = [], [], []

        def norm_two(s):
            normed_own, mid, square = stage(
                norm_two_kernel,
                "norm_two",
                attn[s].parts()
                + [(hidden_r, Dynamic(width, s)), (valid_r, Valid(s)), full(gain_f)],
                [new(quarter, width), new(quarter, width, dtype=F32), new(2, width, dtype=F32)],
                placed=True,
            )
            middle.append(mid)
            squares.append(square)
            two.append(Collect(normed_own))

        two_rows = active = d_gate = d_upper = None

        def units_of(s):
            nonlocal two_rows, active, d_gate, d_upper
            outs = (two_rows, active, d_gate, d_upper)
            two_rows, active, d_gate, d_upper = stage(
                functools.partial(units_kernel, units),
                "units",
                fulls(two[s].got)
                + [(gate_t, by_row(UNITS, width)), (up_t, by_row(UNITS, width))]
                + [(d_active[s], by_col(local, UNITS))],
                [(shape(rows, width), part(width, s))]
                + [(shape(rows, wide), pl.BlockSpec((local, UNITS), lambda i: (s, i)))] * 3,
                grid=pl.cdiv(wide, UNITS),
                shared=outs if s else None,
            )

        for s in every:
            attend(s)
        for s in every:
            attn[s].first()
        for s in every:
            attn[s].second()
        for s in every:
            norm_two(s)
        for s in every:
            two[s].second()
            units_of(s)

        down_sum = Grad((cot_moved, active))
        gate_sum = Grad((two_rows, d_gate))
        up_sum = Grad((two_rows, d_upper))
        gate_sum.away()
        down_sum.away()
        down_sum.send()
        d_two = [
            Spread(*split_columns(s, [d_gate, d_upper], [gate_t, up_t], "d_two")) for s in every
        ]
        for s in every:
            d_two[s].first()
        for s in every:
            d_two[s].second()

        branch, out_squares, out_parts = [], [], []

        def branch_of(s):
            branch.append(Spread(*split_columns(s, [active], [w_down], "branch")))

        def output_of(s):
            value, square = stage(
                output_kernel,
                "output",
                branch[s].parts() + [full(middle[s]), (valid_r, Valid(s))],
                [new(quarter, width), new(1, width, dtype=F32)],
                placed=True,
            )
            out_squares.append(square)
            out_parts.append(Collect(value))

        d_middle, d_low, gain_f_parts = [], [], []

        def middle_back(s):
            low, mid, gains = stage(
                middle_back_kernel,
                "middle_back",
                d_two[s].parts() + [full(middle[s]), (cot_r, Dynamic(width, s)), full(gain_f)],
                [new(quarter, width), new(quarter, width, dtype=F32), new(1, width, dtype=F32)],
                placed=True,
            )
            d_middle.append(mid)
            gain_f_parts.append(gains)
            d_low.append(Collect(low))

        branch_of(0)
        for s in every:
            middle_back(s)
        for s in every[1:]:
            branch_of(s)
        d_low[0].second()
        gate_sum.send(down_sum)
        down_sum.own()
        for s in every[1:]:
            d_low[s].second()
        for s in every:
            branch[s].first()

        d_q_raw, d_pieces, d_rows, passed = [], [], None, None
        gain_q_parts = []

        def attend_back(s):
            nonlocal d_rows
            outs = stage(
                functools.partial(attend_back_kernel, tile, ctx_n, s),
                "attend_back",
                fulls([seg_rows[s], exts[s], mixed[s]] + d_low[s].got + [w_out, q_raw[s]])
                + tables(local)
                + fulls([gq] + pieces[s]),
                [
                    (shape(rows, width), part(width, s)),
                    new(local, q_cols),
                    new(1, q_cols, dtype=F32),
                ]
                + [new(local, 2 * LANES)] * ctx_n,
                scratch=[
                    pltpu.VMEM((heads, local, LANES), BF),
                    pltpu.VMEM((q_cols, local), F32),
                    pltpu.VMEM((local, q_cols), BF),
                ],
                placed=True,
                shared=[d_rows] if s else None,
            )
            d_rows = outs[0]
            d_q_raw.append(outs[1])
            gain_q_parts.append(outs[2])
            d_pieces.append(outs[3:])

        def pass_back(back):
            nonlocal passed
            mine = [d_pieces[s][back] for s in every]
            args = fulls(mine)
            if back < ctx_n - 1:
                args.append(full(passed))
            passed = stage(pass_back_kernel, "pass_back", args, [new(rows, 2 * LANES)])[0]
            passed = lax.ppermute(passed, "ctx", down)

        d_qkv, d_one, gain_k_parts = None, [], []

        def key_back(s):
            nonlocal d_qkv
            d_qkv, *parts, gains = stage(
                key_back_kernel,
                "key_back",
                [
                    full(d_pieces[s][0]),
                    (passed, by_block(local, 2 * LANES, s)),
                    full(d_q_raw[s]),
                    full(k_raw[s]),
                ]
                + tables(local)
                + fulls([gk, w_query, w_key, w_value]),
                [(shape(rows, q_cols + 2 * LANES), part(q_cols + 2 * LANES, s))]
                + parts_out
                + [new(1, LANES, dtype=F32)],
                scratch=[pltpu.VMEM((local, q_cols + 2 * LANES), BF)],
                placed=True,
                shared=[d_qkv] if s else None,
            )
            gain_k_parts.append(gains)
            d_one.append(Spread(*parts))

        gain_a_parts, back_hidden = [], []

        def hidden_back(s):
            grad, gains = stage(
                hidden_back_kernel,
                "hidden_back",
                d_one[s].parts()
                + [(hidden_r, Dynamic(width, s)), full(d_middle[s]), full(gain_a)],
                [new(quarter, width), new(1, width, dtype=F32)],
                placed=True,
            )
            gain_a_parts.append(gains)
            back_hidden.append(Collect(grad))

        def place(parts):
            return stage(
                place_kernel,
                "place",
                fulls([p for c in parts for p in c.got]),
                [new(rows, width)],
                placed=True,
            )[0]

        attend_back(0)
        down_sum.third()
        for s in every:
            branch[s].second()
        for s in every[1:]:
            attend_back(s)
        up_sum.away()
        up_sum.send(gate_sum)
        if ctx_n > 1:
            pass_back(ctx_n - 1)
        gate_sum.own()
        for i, back in enumerate(range(ctx_n - 2, 0, -1)):
            pass_back(back)
            if i == 0:
                for s in every:
                    output_of(s)
        grad_down = down_sum.last()[:, :units].T
        gate_sum.third()
        for s in every:
            out_parts[s].second()
        key_back(0)
        up_sum.wait()
        for s in every[1:]:
            key_back(s)
        for s in every:
            d_one[s].first()
        for s in every:
            d_one[s].second()
        rest_sum = Grad((normed, d_qkv), (d_rows, mixed_moved))
        rest_sum.away()
        rest_sum.send()
        up_sum.own()
        output = place(out_parts).reshape(seqs, local, width)
        for s in every:
            hidden_back(s)
        rest_sum.wait()
        for s in every:
            back_hidden[s].second()
        rest_sum.own()
        grad_gate = gate_sum.last()[:, :units]

        gain_q_part = sum(gain_q_parts).reshape(heads, HEAD).sum(axis=0)
        gain_k_part = sum(gain_k_parts).reshape(2, HEAD).sum(axis=0)
        total_square = sum(squares).sum(axis=1)
        branch_square = sum(out_squares).sum()
        count = jnp.sum(valid).astype(F32) / tp_n
        small = jnp.concatenate(
            [
                sum(gain_a_parts)[0],
                sum(gain_f_parts)[0],
                gain_q_part,
                gain_k_part,
                jnp.stack([total_square[1], total_square[0], branch_square, count]),
                jnp.zeros((LANES - 4,), F32),
            ]
        ).reshape(-1, LANES)
        (small,) = o.tie(small)
        flips = [(a, b) for a in ("tp", "ctx", "dp") for _, b in bits(a, sizes[a])[::-1]]

        def sum_step():
            nonlocal small
            small, got = o.tie(small, swap(small, flips.pop(0)))
            small = o.mark(small + got)

        if flips:
            sum_step()
        grad_hidden = place(back_hidden).reshape(seqs, local, width)
        up_sum.third()
        while flips:
            sum_step()
        rest_sum.third()
        grad_up = up_sum.last()[:, :units]
        grad_rest = rest_sum.last()
        grad_qkv = grad_rest[:, : q_cols + 2 * LANES]
        grad_out = grad_rest[:, q_cols + 2 * LANES :].T

        small = small.reshape(-1)
        at = 2 * width + 2 * HEAD
        denom = jnp.maximum(small[at + 3], 1.0) * width
        root = lambda spot: jnp.sqrt(small[at + spot] / denom)
        return (
            output,
            grad_hidden,
            grad_qkv[:, :q_cols],
            grad_qkv[:, q_cols : q_cols + LANES],
            grad_qkv[:, q_cols + LANES :],
            grad_out,
            grad_gate,
            grad_up,
            grad_down,
            small[:width],
            small[width : 2 * width],
            small[2 * width : 2 * width + HEAD],
            small[2 * width + HEAD : at],
            root(0),
            root(1),
            root(2),
        )

    return body


def solution(mesh):
    tokens = P("dp", "ctx", None)
    marks = P("dp", "ctx")
    columns = P(None, "tp")
    rows = P("tp", None)
    by_rows = P(("dp", "ctx"), "tp")
    by_columns = P("tp", ("dp", "ctx"))
    in_specs = (tokens, tokens, marks, marks, columns, columns, columns, rows)
    in_specs += (columns, columns, rows, P(), P(), P(), P())
    out_specs = (tokens, tokens, by_rows, by_rows, by_rows, by_columns, by_rows, by_rows)
    out_specs += (by_columns, P(), P(), P(), P(), P(), P(), P())
    return jax.shard_map(
        build(mesh), mesh=mesh, in_specs=in_specs, out_specs=out_specs, check_vma=False
    )
```

```python
import functools

import jax
import jax.numpy as jnp
import numpy as np
from jax import lax
from jax.experimental import pallas as pl
from jax.experimental.pallas import tpu as pltpu
from jax.sharding import PartitionSpec as P

HEAD = 64
EPS = 1e-05
THETA = 1000000.0
BF = jnp.bfloat16
F32 = jnp.float32
LANES = 128
VMEM_LIMIT = 56 * 1024 * 1024


def nn_dot(left, right):
    return lax.dot_general(left, right, (((1,), (0,)), ((), ())), preferred_element_type=F32)


def nt_dot(left, right):
    return lax.dot_general(left, right, (((1,), (1,)), ((), ())), preferred_element_type=F32)


def tn_dot(left, right):
    return lax.dot_general(left, right, (((0,), (0,)), ((), ())), preferred_element_type=F32)


def rms_scale(values):
    return lax.rsqrt(jnp.mean(values * values, axis=-1, keepdims=True) + EPS)


def norm_back(grads, unit, scale, gain):
    scaled = grads * gain
    return scale * (scaled - unit * jnp.mean(scaled * unit, axis=-1, keepdims=True))


def lane_of(shape):
    return lax.broadcasted_iota(jnp.int32, shape, len(shape) - 1)


def head_mean(slab):
    row = lax.broadcasted_iota(jnp.int32, (LANES, LANES), 0)
    col = lax.broadcasted_iota(jnp.int32, (LANES, LANES), 1)
    same = jnp.where((row < HEAD) == (col < HEAD), 1.0 / HEAD, 0.0).astype(BF)
    high = slab.astype(BF)
    rest = slab - high.astype(F32)
    mid = rest.astype(BF)
    low = (rest - mid.astype(F32)).astype(BF)
    return nn_dot(high, same) + nn_dot(mid, same) + nn_dot(low, same)


def turn(slab, cosines, sines):
    half = HEAD // 2
    lane = lane_of(slab.shape)
    partner = jnp.where(
        (lane & (HEAD - 1)) < half,
        pltpu.roll(slab, LANES - half, 1),
        pltpu.roll(slab, half, 1),
    )
    return slab * cosines + partner * sines


def with_ones(slab, which):
    wide = slab.astype(F32)
    if which == 1:
        wide = pltpu.roll(wide, HEAD, 1)
    lane = lane_of(wide.shape)
    return jnp.where(lane < HEAD, wide, jnp.where(lane < HEAD + 3, 1.0, 0.0))


def with_minus(low, column):
    first = (-column).astype(BF).astype(F32)
    rest = -column - first
    second = rest.astype(BF).astype(F32)
    third = rest - second
    lane = lane_of(low.shape)
    tail = jnp.where(
        lane == HEAD,
        first,
        jnp.where(lane == HEAD + 1, second, jnp.where(lane == HEAD + 2, third, 0.0)),
    )
    return jnp.where(lane < HEAD, low, tail).astype(BF)


def low_head(ref, head):
    slab = ref[:, (head // 2) * LANES : (head // 2 + 1) * LANES].astype(F32)
    return pltpu.roll(slab, HEAD, 1) if head % 2 else slab


def place_heads(raw, gains, cosines, sines):
    return turn(raw * lax.rsqrt(head_mean(raw * raw) + EPS) * gains, cosines, sines)


def key_value_kernel(spots, hidden, gain, wk, wv, cosines, sines, gain_k, normed, kv, k_raw):
    x = hidden[...].astype(F32)
    rows = (x * rms_scale(x) * gain[...]).astype(BF)
    normed[...] = rows
    key = nn_dot(rows, wk[...])
    k_raw[...] = key
    kv[:, :LANES] = place_heads(key, gain_k[...], cosines[...], sines[...]).astype(BF)
    kv[:, LANES:] = nn_dot(rows, wv[...]).astype(BF)


def query_kernel(spots, normed, wq, cosines, sines, gain_q, query, q_raw):
    raw = nn_dot(normed[...], wq[...])
    q_raw[...] = raw
    for slab in range(raw.shape[1] // LANES):
        at = slice(slab * LANES, (slab + 1) * LANES)
        placed = place_heads(raw[:, at], gain_q[...], cosines[...], sines[...])
        query[:, at] = (placed.astype(BF).astype(F32) * 0.125).astype(BF)


def attend_kernel(tile, seq, spots, seg_row, query, w_out, *refs):
    pieces = refs[:-10]
    moved, *sums = refs[-10:-5]
    mixed, ext, low, total, seg = refs[-5:]
    rows = query.shape[0]
    heads = query.shape[1] // HEAD
    group = heads // 2
    me = spots[4]
    first_doc = spots[5 + seq]
    wide_row = jnp.broadcast_to(seg_row[...].astype(F32), (LANES, rows))
    seg[...] = wide_row.T[:, :1].astype(jnp.int32)
    lane = lane_of((rows, LANES))
    for head in range(heads):
        low[head] = jnp.where(lane < HEAD, low_head(query, head), 0.0).astype(BF)
    total[...] = jnp.zeros_like(total)

    def tile_step(back, block, piece):
        start = (me - back) * rows + block * tile

        @pl.when(start + tile > first_doc)
        def _():
            kv = piece[pl.ds(block * tile, tile), :]
            shape = (rows, tile)
            place = start + lax.broadcasted_iota(jnp.int32, shape, 1)
            allowed = place >= seg[...]
            if back == 0:
                allowed &= place <= me * rows + lax.broadcasted_iota(jnp.int32, shape, 0)
            for which in range(2):
                key = with_ones(kv[:, :LANES], which).astype(BF)
                value = with_ones(kv[:, LANES:], which).astype(BF)
                for head in range(which * group, (which + 1) * group):
                    scores = jnp.where(allowed, nt_dot(low[head], key), -1e30)
                    total[head] += nn_dot(jnp.exp(scores).astype(BF), value)

    for back, piece in enumerate(pieces):

        @pl.when(me >= back)
        def _(back=back, piece=piece):
            def step(block, carry):
                tile_step(back, block, piece)
                return carry

            lax.fori_loop(0, rows // tile, step, 0)

    for slab in range(heads // 2):
        parts = []
        for head in (2 * slab, 2 * slab + 1):
            got = total[head]
            weight = got[:, HEAD : HEAD + 1]
            parts.append(got / weight)
            ext[head] = with_minus(low[head].astype(F32), jnp.log(weight))
        joined = jnp.where(lane < HEAD, parts[0], pltpu.roll(parts[1], HEAD, 1))
        mixed[:, slab * LANES : (slab + 1) * LANES] = joined.astype(BF)
    block = rows // 4
    for i, at in enumerate(spots_of(spots, 4, rows)):
        moved[i * block : (i + 1) * block, :] = mixed[at, :]
    split_rows(nn_dot(moved[...], w_out[...]), *sums)


def attend_back_kernel(
    tile,
    count,
    seq,
    spots,
    seg,
    ext,
    mixed,
    own,
    near,
    far,
    far_near,
    w_out,
    q_raw,
    cosines,
    sines,
    gain_q,
    *refs,
):
    pieces = refs[:count]
    d_rows, d_q_raw, gain_part = refs[count : count + 3]
    d_pieces = refs[count + 3 : 2 * count + 3]
    d_ext, d_query, d_mixed = refs[2 * count + 3 :]
    rows = mixed.shape[0]
    heads = mixed.shape[1] // HEAD
    group = heads // 2
    me = spots[4]
    first_doc = spots[5 + seq]
    lane = lane_of((rows, LANES))
    block = rows // 4
    for i, part in enumerate((own, near, far, far_near)):
        d_rows[i * block : (i + 1) * block, :] = part[...]
    moved = nt_dot(d_rows[...], w_out[...]).astype(BF)
    for i, at in enumerate(spots_of(spots, 4, rows)):
        d_mixed[at, :] = moved[i * block : (i + 1) * block]
    for head in range(heads):
        grad = jnp.where(lane < HEAD, low_head(d_mixed, head), 0.0)
        delta = jnp.sum(grad * low_head(mixed, head), axis=-1, keepdims=True)
        d_ext[head] = with_minus(grad, delta)
    d_query[...] = jnp.zeros_like(d_query)
    low_tile = lane_of((tile, LANES)) < HEAD

    def tile_step(back, block, piece, d_piece):
        start = (me - back) * rows + block * tile
        needed = start + tile > first_doc
        at = pl.ds(block * tile, tile)

        @pl.when(needed)
        def _():
            kv = piece[at, :]
            shape = (tile, rows)
            place = start + lax.broadcasted_iota(jnp.int32, shape, 0)
            allowed = place >= seg[...]
            if back == 0:
                allowed &= place <= me * rows + lax.broadcasted_iota(jnp.int32, shape, 1)
            d_keys = []
            d_values = []
            for which in range(2):
                key_f = with_ones(kv[:, :LANES], which)
                key = key_f.astype(BF)
                key_t = key_f.T[:HEAD].astype(BF)
                value = with_ones(kv[:, LANES:], which).astype(BF)
                d_key = jnp.zeros((tile, LANES), F32)
                d_value = jnp.zeros((tile, LANES), F32)
                for head in range(which * group, (which + 1) * group):
                    scores = jnp.where(allowed, nt_dot(key, ext[head]), -1e30)
                    probs = jnp.exp(scores)
                    d_scores = (probs * nt_dot(value, d_ext[head])).astype(BF)
                    d_value += nn_dot(probs.astype(BF), d_ext[head])
                    d_key += nn_dot(d_scores, ext[head])
                    d_query[head * HEAD : (head + 1) * HEAD, :] += nn_dot(key_t, d_scores)
                d_keys.append(d_key)
                d_values.append(d_value)
            for spot, pair in enumerate((d_keys, d_values)):
                joined = jnp.where(low_tile, pair[0], pltpu.roll(pair[1], HEAD, 1))
                d_piece[at, spot * LANES : (spot + 1) * LANES] = joined.astype(BF)

        @pl.when(jnp.logical_not(needed))
        def _():
            d_piece[at, :] = jnp.zeros((tile, 2 * LANES), BF)

    for back, (piece, d_piece) in enumerate(zip(pieces, d_pieces)):

        @pl.when(me >= back)
        def _(back=back, piece=piece, d_piece=d_piece):
            def step(block, carry):
                tile_step(back, block, piece, d_piece)
                return carry

            lax.fori_loop(0, rows // tile, step, 0)

        @pl.when(me < back)
        def _(d_piece=d_piece):
            d_piece[...] = jnp.zeros_like(d_piece)

    for slab in range(heads // 2):
        at = slice(slab * LANES, (slab + 1) * LANES)
        grad = (d_query[at, :].T * 0.125).astype(BF).astype(F32)
        out, part = rope_norm_back(grad, q_raw[:, at], cosines[...], sines[...], gain_q[...])
        d_q_raw[:, at] = out
        gain_part[:, at] = part


def rope_norm_back(grad, raw, cosines, sines, gains):
    back = turn(grad, cosines, -sines)
    scale = lax.rsqrt(head_mean(raw * raw) + EPS)
    unit = raw * scale
    scaled = back * gains
    out = scale * (scaled - unit * head_mean(scaled * unit))
    part = jnp.sum(back * unit, axis=0, keepdims=True)
    return out.astype(BF), part


def key_back_kernel(
    quarters,
    d_piece,
    got,
    d_q_raw,
    k_raw,
    cosines,
    sines,
    gain_k,
    w_query,
    w_key,
    w_value,
    d_qkv,
    own,
    near,
    far,
    far_near,
    gain_part,
    moved,
):
    q_cols = d_q_raw.shape[1]
    total = (d_piece[...].astype(F32) + got[...].astype(F32)).astype(BF)
    d_key = total[:, :LANES].astype(F32)
    out, part = rope_norm_back(d_key, k_raw[...], cosines[...], sines[...], gain_k[...])
    gain_part[...] = part
    d_qkv[:, :q_cols] = d_q_raw[...]
    d_qkv[:, q_cols : q_cols + LANES] = out
    d_qkv[:, q_cols + LANES :] = total[:, LANES:]
    block = moved.shape[0] // 4
    for i, at in enumerate(spots_of(quarters, 4, moved.shape[0])):
        moved[i * block : (i + 1) * block, :] = d_qkv[at, :]
    grad = nt_dot(moved[:, :q_cols], w_query[...])
    grad += nt_dot(moved[:, q_cols : q_cols + LANES], w_key[...])
    grad += nt_dot(moved[:, q_cols + LANES :], w_value[...])
    split_rows(grad, own, near, far, far_near)


def spots_of(spots, count, rows, skip=0):
    block = rows // count
    return [pl.ds(pl.multiple_of(spots[skip + i] * block, 16), block) for i in range(count)]


def split_rows(total, *parts):
    block = total.shape[0] // len(parts)
    for i, part in enumerate(parts):
        part[...] = total[i * block : (i + 1) * block].astype(part.dtype)


def d_active_kernel(quarters, rows, right, moved, out):
    @pl.when(pl.program_id(0) == 0)
    def _():
        block = rows.shape[0] // 4
        for i, at in enumerate(spots_of(quarters, 4, rows.shape[0])):
            moved[i * block : (i + 1) * block, :] = rows[at, :]

    out[...] = nt_dot(moved[...], right[...]).astype(BF)


def units_kernel(
    units, own, near, far, far_near, gate_t, up_t, d_active, rows, active, d_gate, d_upper
):
    @pl.when(pl.program_id(0) == 0)
    def _():
        block = own.shape[0]
        for i, part in enumerate((own, near, far, far_near)):
            rows[i * block : (i + 1) * block, :] = part[...]

    x = rows[...]
    wide = active.shape[1]
    half = wide // 2
    for part in range(2):
        at = slice(part * half, (part + 1) * half)
        gate = nt_dot(x, gate_t[at, :])
        upper = nt_dot(x, up_t[at, :])
        column = pl.program_id(0) * wide + part * half + lane_of(gate.shape)
        real = column < units
        sigma = jax.nn.sigmoid(gate)
        silu = gate * sigma
        grad = d_active[:, at].astype(F32)
        active[:, at] = jnp.where(real, silu * upper, 0.0).astype(BF)
        d_upper[:, at] = jnp.where(real, grad * silu, 0.0).astype(BF)
        slope = grad * upper * (sigma + silu * (1.0 - sigma))
        d_gate[:, at] = jnp.where(real, slope, 0.0).astype(BF)


def columns_kernel(count, *refs):
    depth = refs[count].shape[0]
    total = sum(nn_dot(refs[i][:, :depth], refs[count + i][...]) for i in range(count))
    split_rows(total, *refs[2 * count :])


def masked_sum(valid, values):
    mask = jnp.broadcast_to(valid[0].astype(F32), (8, values.shape[0]))
    total = lax.dot_general(
        mask,
        values,
        (((1,), (0,)), ((), ())),
        precision=lax.Precision.HIGHEST,
        preferred_element_type=F32,
    )
    return total[:1]


def pass_back_kernel(first, second, *refs):
    out = refs[-1]
    local = first.shape[0]
    for i, part in enumerate((first, second)):
        at = slice(i * local, (i + 1) * local)
        if len(refs) > 1:
            out[at, :] = (part[...].astype(F32) + refs[0][at, :].astype(F32)).astype(BF)
        else:
            out[at, :] = part[...]


def norm_two_kernel(spot, kept, got_far, got, hidden, valid, gain, normed, middle, squares):
    attn = kept[...] + got_far[...].astype(F32) + got[...].astype(F32)
    before = hidden[...].astype(F32)
    total = before + attn
    middle[...] = total
    normed[...] = (total * rms_scale(total) * gain[...]).astype(BF)
    squares[0:1, :] = masked_sum(valid, attn * attn)
    squares[1:2, :] = masked_sum(valid, before * before)


def middle_back_kernel(spot, kept, got_far, got, middle, cot, gain, d_low, d_middle, gain_part):
    grad = kept[...] + got_far[...].astype(F32) + got[...].astype(F32)
    before = middle[...]
    scale = rms_scale(before)
    unit = before * scale
    gain_part[...] = jnp.sum(grad * unit, axis=0, keepdims=True)
    total = cot[...].astype(F32) + norm_back(grad, unit, scale, gain[...])
    d_middle[...] = total
    d_low[...] = total.astype(BF)


def hidden_back_kernel(spot, kept, got_far, got, hidden, d_middle, gain, out, gain_part):
    grad = kept[...] + got_far[...].astype(F32) + got[...].astype(F32)
    before = hidden[...].astype(F32)
    scale = rms_scale(before)
    unit = before * scale
    gain_part[...] = jnp.sum(grad * unit, axis=0, keepdims=True)
    out[...] = (d_middle[...] + norm_back(grad, unit, scale, gain[...])).astype(BF)


def output_kernel(spot, kept, got_far, got, middle, valid, out, squares):
    branch = kept[...] + got_far[...].astype(F32) + got[...].astype(F32)
    out[...] = (middle[...] + branch).astype(BF)
    squares[...] = masked_sum(valid, branch * branch)


def place_kernel(quarters, *refs):
    parts, out = refs[:-1], refs[-1]
    block = parts[0].shape[0]
    for i, part in enumerate(parts):
        first = pl.multiple_of((i // 4 * 4 + quarters[i % 4]) * block, 16)
        out[pl.ds(first, block), :] = part[...]


def rope_tables(length):
    places = np.arange(length).astype(np.float32)
    half = HEAD // 2
    freqs = np.float32(THETA) ** (-np.arange(half).astype(np.float32) / np.float32(half))
    angles = (places[:, None] * freqs.astype(np.float32)[None, :]).astype(np.float64)
    cosines = np.cos(angles).astype(np.float32)
    sines = np.sin(angles).astype(np.float32)
    return (
        np.concatenate([cosines] * 4, axis=1),
        np.concatenate([-sines, sines, -sines, sines], axis=1),
    )


def after(value, *others):
    return lax.optimization_barrier((value,) + others)[0]


def params():
    return pltpu.CompilerParams(vmem_limit_bytes=VMEM_LIMIT)


def call(kernel, name, **kw):
    small = pl.CostEstimate(flops=1, bytes_accessed=1, transcendentals=0)
    return pl.pallas_call(kernel, compiler_params=params(), cost_estimate=small, name=name, **kw)


def shape(*dims, dtype=BF):
    return jax.ShapeDtypeStruct(dims, dtype)


def fixed(*dims):
    return pl.BlockSpec(dims, lambda i: (0,) * len(dims))


def by_row(rows, cols, first=0):
    return pl.BlockSpec((rows, cols), lambda i: (first + i, 0))


def by_block(rows, cols, spot):
    return pl.BlockSpec((rows, cols), lambda i: (spot, 0))


def by_col(rows, cols):
    return pl.BlockSpec((rows, cols), lambda i: (0, i))


SMEM = pl.BlockSpec(memory_space=pltpu.SMEM)
UNITS = 512
PAD = 256


def flip(n, bit):
    return [(i, i ^ bit) for i in range(n)]


def cut(array, start, size):
    return lax.dynamic_slice_in_dim(array, start, size, axis=0)


class Order:
    def __init__(self):
        self.last = None

    def tie(self, *values):
        if self.last is not None:
            values = lax.optimization_barrier(values + (self.last,))[:-1]
        return values

    def mark(self, value):
        self.last = value
        return value

    def wait(self, values, spot):
        values[spot] = self.mark(self.tie(values[spot])[0])


def build(mesh):
    dp_n, ctx_n, tp_n = (mesh.shape[a] for a in ("dp", "ctx", "tp"))
    blocks = dp_n * ctx_n

    def bits(axis, n):
        out = []
        while n > 1:
            n //= 2
            out.append((axis, n))
        return out

    steps = bits("dp", dp_n) + bits("ctx", ctx_n)[::-1]
    sizes = {"dp": dp_n, "ctx": ctx_n, "tp": tp_n}

    def swap(value, step):
        axis, bit = step
        return lax.ppermute(value, axis, flip(sizes[axis], bit))

    core, across = ("tp", 1), ("tp", 2)

    def bit_of(step):
        axis, bit = step
        return lax.axis_index(axis) // bit % 2

    def halves(part, step, outer):
        axis, bit = step
        left = 1 if axis == "dp" else outer * ctx_n // (2 * bit)
        view = part.reshape(left, 2, -1, part.shape[-1])
        mine = bit_of(step)
        pick = lambda which: lax.dynamic_index_in_dim(view, which, 1, keepdims=False).reshape(
            -1, part.shape[-1]
        )
        return pick(mine), pick(1 - mine)

    def body(
        hidden,
        cotangent,
        segments,
        valid,
        w_query,
        w_key,
        w_value,
        w_out,
        w_gate,
        w_up,
        w_down,
        gain_attn,
        gain_ffn,
        gain_query,
        gain_key,
    ):
        seqs, local, width = hidden.shape
        rows = seqs * local
        every = range(seqs)
        q_cols = w_query.shape[1]
        units = w_gate.shape[1]
        wide = pl.cdiv(units, PAD) * PAD
        heads = q_cols // HEAD
        me = lax.axis_index("ctx")
        member = lax.axis_index("tp")
        o = Order()
        cosines, sines = (jnp.asarray(t) for t in rope_tables(local * ctx_n))
        hidden_r = hidden.reshape(rows, width)
        cot_r = cotangent.reshape(rows, width)
        valid_r = valid.reshape(seqs * 4, 1, local // 4)
        gate_t, up_t = w_gate.T, w_up.T
        gq = jnp.concatenate([gain_query, gain_query])[None]
        gk = jnp.concatenate([gain_key, gain_key])[None]
        gain_a, gain_f = gain_attn[None], gain_ffn[None]
        tile = 256
        half, quarter = local // 2, local // 4
        own = (member % 2) * 2 + member // 2
        spots = jnp.stack([own ^ i for i in range(4)] + [me])
        spots = jnp.concatenate([spots, segments[:, 0]]).astype(jnp.int32)
        seg_rows = [segments[s][None] for s in every]
        _, *seg_rows = lax.optimization_barrier((spots, *seg_rows))

        def stage(kernel, name, args, outs, grid=1, scratch=(), placed=False, shared=None):
            arrays = [a for a, _ in args]
            arrays[:1] = o.tie(arrays[0])
            fix = lambda spec: pl.BlockSpec(spec.block_shape, lambda i, *s: spec.index_map(i))
            of = lambda spec: spec.spec if isinstance(spec, Dynamic) else fix(spec)
            specs = [of(spec) for _, spec in args]
            old = list(shared or [])
            count = int(placed) + len(args)
            run = kernel
            if old:
                run = lambda *refs: kernel(*refs[:count], *refs[count + len(old) :])
            got = pl.pallas_call(
                run,
                grid_spec=pltpu.PrefetchScalarGridSpec(
                    num_scalar_prefetch=int(placed),
                    grid=(grid,),
                    in_specs=specs + [pl.BlockSpec(memory_space=pl.ANY)] * len(old),
                    out_specs=[fix(s) for _, s in outs],
                    scratch_shapes=list(scratch),
                ),
                out_shape=[s for s, _ in outs],
                input_output_aliases={count + i: i for i in range(len(old))},
                compiler_params=params(),
                cost_estimate=pl.CostEstimate(flops=1, bytes_accessed=1, transcendentals=0),
                name=name,
            )(*([spots] if placed else []), *arrays, *old)
            o.mark(got[0])
            return got

        class Dynamic:
            def __init__(self, cols, seq):
                self.spec = pl.BlockSpec((quarter, cols), lambda i, s: (seq * 4 + s[0], 0))

        def full(array):
            return (array, fixed(*array.shape))

        def fulls(arrays):
            return [full(a) for a in arrays]

        def new(*dims, dtype=BF):
            return (shape(*dims, dtype=dtype), fixed(*dims))

        def part(cols, s):
            return by_block(local, cols, s)

        class Table(Dynamic):
            def __init__(self, rows):
                per = local // rows
                self.spec = pl.BlockSpec((rows, LANES), lambda i, s: (s[4] * per + i, 0))

        class Valid(Dynamic):
            def __init__(self, seq):
                self.spec = pl.BlockSpec((1, 1, quarter), lambda i, s: (seq * 4 + s[0], 0, 0))

        tables = lambda n: [(t, Table(n)) for t in (cosines, sines)]

        parts_out = [
            (shape(quarter, width, dtype=d), fixed(quarter, width)) for d in (F32, F32, BF, BF)
        ]

        def split_columns(s, lefts, rights, name):
            count = len(lefts)
            depth, cols = rights[0].shape
            return stage(
                functools.partial(columns_kernel, count),
                name,
                [(l, part(l.shape[1], s)) for l in lefts] + [(r, by_col(depth, UNITS)) for r in rights],
                [(out, by_col(quarter, UNITS)) for out, _ in parts_out],
                grid=cols // UNITS,
            )

        class Spread:
            def __init__(self, own, near, far, far_near):
                self.own, self.near = own, near
                self.far = [far_near, far]

            def first(self):
                self.far = list(o.tie(*self.far))
                o.mark(self.far[0])
                self.got = [swap(f, core) for f in self.far]

            def second(self):
                near, got = o.tie(self.near, self.got[0])
                away = o.mark((near + got.astype(F32)).astype(BF))
                self.got[0] = swap(away, across)

            def parts(self):
                return fulls([self.own, self.got[1], self.got[0]])

        class Collect:
            def __init__(self, mine):
                self.got = [mine, swap(mine, across)]

            def second(self):
                o.wait(self.got, 1)
                self.got += [swap(value, core) for value in self.got]

        half_of = lambda left, which: lax.dynamic_slice_in_dim(
            left, which * (width // 2), width // 2, axis=1
        )

        def other_ctx(left, which):
            view = left.reshape(rows, blocks // 2, 2, width // blocks)
            return lax.dynamic_index_in_dim(view, which, 2, keepdims=False).reshape(rows, -1)

        class Grad:
            def __init__(self, *pairs, ctx_first=False):
                dp_bits = [step for step in steps if step[0] == "dp"]
                ctx_bits = [step for step in steps if step[0] == "ctx"]
                self.steps = ctx_bits + dp_bits if ctx_first else dp_bits + ctx_bits
                self.outer = dp_n if ctx_first else 1
                pick = other_ctx if ctx_first else half_of
                bit = bit_of(self.steps[0])
                self.rights = [right for _, right in pairs]
                self.keep = [lambda left=left: pick(left, bit) for left, _ in pairs]
                self.give = [lambda left=left: pick(left, 1 - bit) for left, _ in pairs]

            def away(self):
                rights = o.tie(*self.rights)
                parts = [tn_dot(left(), r).astype(BF) for left, r in zip(self.give, rights)]
                self.out = o.mark(jnp.concatenate(parts, axis=1))

            def send(self, *waits):
                for grad in waits:
                    grad.wait()
                (out,) = o.tie(self.out)
                self.got = swap(o.mark(out), self.steps[0])
                self.left_steps = self.steps[1:]

            def wait(self):
                (self.got,) = o.tie(self.got)
                o.mark(self.got)

            def columns(self, got):
                ends = np.cumsum([r.shape[1] for r in self.rights])
                return [got[:, e - r.shape[1] : e] for r, e in zip(self.rights, ends)]

            def own(self):
                *rights, got = o.tie(*self.rights, self.got)
                self.terms = []
                for left, r, g in zip(self.keep, rights, self.columns(got)):
                    self.terms.append([o.mark(tn_dot(left(), r) + g.astype(F32))])
                self.pass_on()

            def pass_on(self):
                if not self.left_steps:
                    return
                step = self.left_steps.pop(0)
                stay, away = [], []
                for terms in self.terms:
                    pairs = [halves(t, step, self.outer) for t in terms]
                    stay.append([p[0] for p in pairs])
                    away.append(sum(p[1].astype(F32) for p in pairs).astype(BF))
                got = swap(o.mark(jnp.concatenate(away, axis=1)), step)
                self.terms = [t + [g] for t, g in zip(stay, self.columns(got))]

            def arrive(self):
                for terms in self.terms:
                    (terms[-1],) = o.tie(terms[-1])

            def third(self):
                self.arrive()
                self.pass_on()

            def last(self):
                while self.left_steps:
                    self.third()
                self.arrive()
                return [o.mark(sum(t.astype(F32) for t in terms)) for terms in self.terms]

        up = lambda hops: [(i, i + hops) for i in range(ctx_n - hops)]
        down = [(i + 1, i) for i in range(ctx_n - 1)]
        normed, k_raw, pieces = None, [], []
        step = 256
        per = local // step

        class Around(Dynamic):
            def __init__(self):
                self.spec = pl.BlockSpec((step, LANES), lambda i, s: (s[4] * per + i % per, 0))

        for s in every:
            normed, sent, raw = stage(
                key_value_kernel,
                "key_value",
                [(hidden_r, by_row(step, width, s * per))]
                + fulls([gain_a, w_key, w_value])
                + tables(step)
                + fulls([gk]),
                [
                    (shape(rows, width), by_row(step, width, s * per)),
                    (shape(local, 2 * LANES), by_row(step, 2 * LANES)),
                    (shape(local, LANES, dtype=F32), by_row(step, LANES)),
                ],
                grid=per,
                placed=True,
                shared=[normed] if s else None,
            )
            k_raw.append(raw)
            pieces.append([sent])

        def send_keys(s, direct):
            for hops in range(1, ctx_n if direct else min(3, ctx_n)):
                pieces[s].append(lax.ppermute(pieces[s][0], "ctx", up(hops)))

        for s in every:
            send_keys(s, s > 0)
        query, q_raw = stage(
            query_kernel,
            "query",
            [(normed, by_row(step, width)), full(w_query)]
            + [(t, Around()) for t in (cosines, sines)]
            + fulls([gq]),
            [(shape(rows, q_cols, dtype=d), by_row(step, q_cols)) for d in (BF, F32)],
            grid=seqs * per,
            placed=True,
        )
        d_active, cot_moved = [], None

        def d_active_of(s):
            nonlocal cot_moved
            cot_moved, grad = stage(
                d_active_kernel,
                "d_active",
                [(cot_r, part(width, s)), (w_down, by_row(UNITS, width))],
                [
                    (shape(rows, width), part(width, s)),
                    (shape(local, wide), by_col(local, UNITS)),
                ],
                grid=pl.cdiv(wide, UNITS),
                placed=True,
                shared=[cot_moved] if s else None,
            )
            d_active.append(grad)

        d_active_of(0)
        for spot in range(1, len(pieces[0])):
            o.wait(pieces[0], spot)
        for _ in range(3, ctx_n):
            pieces[0].append(lax.ppermute(pieces[0][-1], "ctx", up(1)))
        for s in every[1:]:
            d_active_of(s)

        mixed, mixed_moved, exts, attn = [], None, [], []

        def attend(s):
            nonlocal mixed_moved
            mixed_moved, *parts, mix, ext = stage(
                functools.partial(attend_kernel, tile, s),
                "attend",
                [full(seg_rows[s]), (query, part(q_cols, s))] + fulls([w_out] + pieces[s]),
                [(shape(rows, q_cols), part(q_cols, s))]
                + parts_out
                + [new(local, q_cols), new(heads, local, LANES)],
                scratch=[
                    pltpu.VMEM((heads, local, LANES), BF),
                    pltpu.VMEM((heads, local, LANES), F32),
                    pltpu.VMEM((local, 1), jnp.int32),
                ],
                placed=True,
                shared=[mixed_moved] if s else None,
            )
            mixed.append(mix)
            exts.append(ext)
            attn.append(Spread(*parts))

        middle, squares, two = [], [], []

        def norm_two(s):
            normed_own, mid, square = stage(
                norm_two_kernel,
                "norm_two",
                attn[s].parts()
                + [(hidden_r, Dynamic(width, s)), (valid_r, Valid(s)), full(gain_f)],
                [new(quarter, width), new(quarter, width, dtype=F32), new(2, width, dtype=F32)],
                placed=True,
            )
            middle.append(mid)
            squares.append(square)
            two.append(Collect(normed_own))

        two_rows = active = d_gate = d_upper = None

        def units_of(s):
            nonlocal two_rows, active, d_gate, d_upper
            outs = (two_rows, active, d_gate, d_upper)
            two_rows, active, d_gate, d_upper = stage(
                functools.partial(units_kernel, units),
                "units",
                fulls(two[s].got)
                + [(gate_t, by_row(UNITS, width)), (up_t, by_row(UNITS, width))]
                + [(d_active[s], by_col(local, UNITS))],
                [(shape(rows, width), part(width, s))]
                + [(shape(rows, wide), pl.BlockSpec((local, UNITS), lambda i: (s, i)))] * 3,
                grid=pl.cdiv(wide, UNITS),
                shared=outs if s else None,
            )

        for s in every:
            attend(s)
        for s in every:
            attn[s].first()
        for s in every:
            attn[s].second()
        for s in every:
            norm_two(s)
        for s in every:
            two[s].second()
            units_of(s)

        down_sum = Grad((cot_moved, active))
        gate_sum = Grad((two_rows, d_gate))
        up_sum = Grad((two_rows, d_upper))
        gate_sum.away()
        down_sum.away()
        down_sum.send()
        d_two = [
            Spread(*split_columns(s, [d_gate, d_upper], [gate_t, up_t], "d_two")) for s in every
        ]
        for s in every:
            d_two[s].first()
        for s in every:
            d_two[s].second()

        branch, out_squares, out_parts = [], [], []

        def branch_of(s):
            branch.append(Spread(*split_columns(s, [active], [w_down], "branch")))

        def output_of(s):
            value, square = stage(
                output_kernel,
                "output",
                branch[s].parts() + [full(middle[s]), (valid_r, Valid(s))],
                [new(quarter, width), new(1, width, dtype=F32)],
                placed=True,
            )
            out_squares.append(square)
            out_parts.append(Collect(value))

        d_middle, d_low, gain_f_parts = [], [], []

        def middle_back(s):
            low, mid, gains = stage(
                middle_back_kernel,
                "middle_back",
                d_two[s].parts() + [full(middle[s]), (cot_r, Dynamic(width, s)), full(gain_f)],
                [new(quarter, width), new(quarter, width, dtype=F32), new(1, width, dtype=F32)],
                placed=True,
            )
            d_middle.append(mid)
            gain_f_parts.append(gains)
            d_low.append(Collect(low))

        branch_of(0)
        for s in every:
            middle_back(s)
        for s in every[1:]:
            branch_of(s)
        d_low[0].second()
        down_sum.wait()
        up_sum.away()
        gate_sum.send()
        down_sum.own()
        for s in every[1:]:
            d_low[s].second()
        for s in every:
            branch[s].first()

        d_q_raw, d_pieces, d_rows, passed = [], [], None, None
        gain_q_parts = []

        def attend_back(s):
            nonlocal d_rows
            outs = stage(
                functools.partial(attend_back_kernel, tile, ctx_n, s),
                "attend_back",
                fulls([seg_rows[s], exts[s], mixed[s]] + d_low[s].got + [w_out])
                + [(q_raw, part(q_cols, s))]
                + tables(local)
                + fulls([gq] + pieces[s]),
                [
                    (shape(rows, width), part(width, s)),
                    new(local, q_cols),
                    new(1, q_cols, dtype=F32),
                ]
                + [new(local, 2 * LANES)] * ctx_n,
                scratch=[
                    pltpu.VMEM((heads, local, LANES), BF),
                    pltpu.VMEM((q_cols, local), F32),
                    pltpu.VMEM((local, q_cols), BF),
                ],
                placed=True,
                shared=[d_rows] if s else None,
            )
            d_rows = outs[0]
            d_q_raw.append(outs[1])
            gain_q_parts.append(outs[2])
            d_pieces.append(outs[3:])

        def pass_back(back):
            nonlocal passed
            mine = [d_pieces[s][back] for s in every]
            args = fulls(mine)
            if back < ctx_n - 1:
                args.append(full(passed))
            passed = stage(pass_back_kernel, "pass_back", args, [new(rows, 2 * LANES)])[0]
            passed = lax.ppermute(passed, "ctx", down)

        d_qkv, d_one, gain_k_parts = None, [], []

        def key_back(s):
            nonlocal d_qkv
            d_qkv, *parts, gains = stage(
                key_back_kernel,
                "key_back",
                [
                    full(d_pieces[s][0]),
                    (passed, by_block(local, 2 * LANES, s)),
                    full(d_q_raw[s]),
                    full(k_raw[s]),
                ]
                + tables(local)
                + fulls([gk, w_query, w_key, w_value]),
                [(shape(rows, q_cols + 2 * LANES), part(q_cols + 2 * LANES, s))]
                + parts_out
                + [new(1, LANES, dtype=F32)],
                scratch=[pltpu.VMEM((local, q_cols + 2 * LANES), BF)],
                placed=True,
                shared=[d_qkv] if s else None,
            )
            gain_k_parts.append(gains)
            d_one.append(Spread(*parts))

        gain_a_parts, back_hidden = [], []

        def hidden_back(s):
            grad, gains = stage(
                hidden_back_kernel,
                "hidden_back",
                d_one[s].parts()
                + [(hidden_r, Dynamic(width, s)), full(d_middle[s]), full(gain_a)],
                [new(quarter, width), new(1, width, dtype=F32)],
                placed=True,
            )
            gain_a_parts.append(gains)
            back_hidden.append(Collect(grad))

        def place(parts):
            return stage(
                place_kernel,
                "place",
                fulls([p for c in parts for p in c.got]),
                [new(rows, width)],
                placed=True,
            )[0]

        attend_back(0)
        for s in every:
            branch[s].second()
        down_sum.third()
        for s in every[1:]:
            attend_back(s)
        up_sum.send(gate_sum)
        if ctx_n > 1:
            pass_back(ctx_n - 1)
        (grad_down,) = down_sum.last()
        for i, back in enumerate(range(ctx_n - 2, 0, -1)):
            pass_back(back)
            if i == 0:
                for s in every:
                    output_of(s)
        gate_sum.own()
        for s in every:
            out_parts[s].second()
        for s in every:
            key_back(s)
        for s in every:
            d_one[s].first()
        rest_sum = Grad((normed, d_qkv), (d_rows, mixed_moved))
        rest_sum.away()
        rest_sum.send(up_sum)
        for s in every:
            d_one[s].second()
        up_sum.own()
        gate_sum.third()
        output = place(out_parts).reshape(seqs, local, width)
        for s in every:
            hidden_back(s)
        rest_sum.wait()
        rest_sum.own()
        for s in every:
            back_hidden[s].second()
        (grad_gate,) = gate_sum.last()

        gain_q_part = sum(gain_q_parts).reshape(heads, HEAD).sum(axis=0)
        gain_k_part = sum(gain_k_parts).reshape(2, HEAD).sum(axis=0)
        total_square = sum(squares).sum(axis=1)
        branch_square = sum(out_squares).sum()
        count = jnp.sum(valid).astype(F32) / tp_n
        small = jnp.concatenate(
            [
                sum(gain_a_parts)[0],
                sum(gain_f_parts)[0],
                gain_q_part,
                gain_k_part,
                jnp.stack([total_square[1], total_square[0], branch_square, count]),
                jnp.zeros((LANES - 4,), F32),
            ]
        ).reshape(-1, LANES)
        (small,) = o.tie(small)
        flips = [(a, b) for a in ("tp", "dp", "ctx") for _, b in bits(a, sizes[a])[::-1]]

        def sum_step():
            nonlocal small
            small, got = o.tie(small, swap(small, flips.pop(0)))
            small = o.mark(small + got)

        ctx_flips = sum(1 for axis, _ in flips if axis == "ctx")
        while len(flips) > ctx_flips:
            sum_step()
        up_sum.third()
        grad_hidden = place(back_hidden).reshape(seqs, local, width)
        while len(flips) > 1:
            sum_step()
        rest_sum.third()
        (grad_up,) = up_sum.last()
        while flips:
            sum_step()
        grad_qkv, grad_out = rest_sum.last()
        grad_down, grad_gate, grad_up = (g[:, :units] for g in (grad_down, grad_gate, grad_up))
        grad_down, grad_out = grad_down.T, grad_out.T

        small = small.reshape(-1)
        at = 2 * width + 2 * HEAD
        denom = jnp.maximum(small[at + 3], 1.0) * width
        root = lambda spot: jnp.sqrt(small[at + spot] / denom)
        return (
            output,
            grad_hidden,
            grad_qkv[:, :q_cols],
            grad_qkv[:, q_cols : q_cols + LANES],
            grad_qkv[:, q_cols + LANES :],
            grad_out,
            grad_gate,
            grad_up,
            grad_down,
            small[:width],
            small[width : 2 * width],
            small[2 * width : 2 * width + HEAD],
            small[2 * width + HEAD : at],
            root(0),
            root(1),
            root(2),
        )

    return body


def solution(mesh):
    tokens = P("dp", "ctx", None)
    marks = P("dp", "ctx")
    columns = P(None, "tp")
    rows = P("tp", None)
    by_rows = P(("dp", "ctx"), "tp")
    by_columns = P("tp", ("dp", "ctx"))
    in_specs = (tokens, tokens, marks, marks, columns, columns, columns, rows)
    in_specs += (columns, columns, rows, P(), P(), P(), P())
    out_specs = (tokens, tokens, by_rows, by_rows, by_rows, by_columns, by_rows, by_rows)
    out_specs += (by_columns, P(), P(), P(), P(), P(), P(), P())
    return jax.shard_map(
        build(mesh), mesh=mesh, in_specs=in_specs, out_specs=out_specs, check_vma=False
    )
```

```python
import functools

import jax
import jax.numpy as jnp
import numpy as np
from jax import lax
from jax.experimental import pallas as pl
from jax.experimental.pallas import tpu as pltpu
from jax.sharding import PartitionSpec as P

HEAD = 64
EPS = 1e-05
THETA = 1000000.0
BF = jnp.bfloat16
F32 = jnp.float32
LANES = 128
VMEM_LIMIT = 56 * 1024 * 1024


def nn_dot(left, right):
    return lax.dot_general(left, right, (((1,), (0,)), ((), ())), preferred_element_type=F32)


def nt_dot(left, right):
    return lax.dot_general(left, right, (((1,), (1,)), ((), ())), preferred_element_type=F32)


def tn_dot(left, right):
    return lax.dot_general(left, right, (((0,), (0,)), ((), ())), preferred_element_type=F32)


def rms_scale(values):
    return lax.rsqrt(jnp.mean(values * values, axis=-1, keepdims=True) + EPS)


def norm_back(grads, unit, scale, gain):
    scaled = grads * gain
    return scale * (scaled - unit * jnp.mean(scaled * unit, axis=-1, keepdims=True))


def lane_of(shape):
    return lax.broadcasted_iota(jnp.int32, shape, len(shape) - 1)


def head_mean(slab):
    row = lax.broadcasted_iota(jnp.int32, (LANES, LANES), 0)
    col = lax.broadcasted_iota(jnp.int32, (LANES, LANES), 1)
    same = jnp.where((row < HEAD) == (col < HEAD), 1.0 / HEAD, 0.0).astype(BF)
    high = slab.astype(BF)
    rest = slab - high.astype(F32)
    mid = rest.astype(BF)
    low = (rest - mid.astype(F32)).astype(BF)
    return nn_dot(high, same) + nn_dot(mid, same) + nn_dot(low, same)


def turn(slab, cosines, sines):
    half = HEAD // 2
    lane = lane_of(slab.shape)
    partner = jnp.where(
        (lane & (HEAD - 1)) < half,
        pltpu.roll(slab, LANES - half, 1),
        pltpu.roll(slab, half, 1),
    )
    return slab * cosines + partner * sines


def with_ones(slab, which):
    wide = slab.astype(F32)
    if which == 1:
        wide = pltpu.roll(wide, HEAD, 1)
    lane = lane_of(wide.shape)
    return jnp.where(lane < HEAD, wide, jnp.where(lane < HEAD + 3, 1.0, 0.0))


def with_minus(low, column):
    first = (-column).astype(BF).astype(F32)
    rest = -column - first
    second = rest.astype(BF).astype(F32)
    third = rest - second
    lane = lane_of(low.shape)
    tail = jnp.where(
        lane == HEAD,
        first,
        jnp.where(lane == HEAD + 1, second, jnp.where(lane == HEAD + 2, third, 0.0)),
    )
    return jnp.where(lane < HEAD, low, tail).astype(BF)


def low_head(ref, head):
    slab = ref[:, (head // 2) * LANES : (head // 2 + 1) * LANES].astype(F32)
    return pltpu.roll(slab, HEAD, 1) if head % 2 else slab


def place_heads(raw, gains, cosines, sines):
    return turn(raw * lax.rsqrt(head_mean(raw * raw) + EPS) * gains, cosines, sines)


def key_value_kernel(spots, hidden, gain, wk, wv, cosines, sines, gain_k, normed, kv, k_raw):
    x = hidden[...].astype(F32)
    rows = (x * rms_scale(x) * gain[...]).astype(BF)
    normed[...] = rows
    key = nn_dot(rows, wk[...])
    k_raw[...] = key
    kv[:, :LANES] = place_heads(key, gain_k[...], cosines[...], sines[...]).astype(BF)
    kv[:, LANES:] = nn_dot(rows, wv[...]).astype(BF)


def query_kernel(spots, normed, wq, cosines, sines, gain_q, query, q_raw):
    raw = nn_dot(normed[...], wq[...])
    q_raw[...] = raw
    for slab in range(raw.shape[1] // LANES):
        at = slice(slab * LANES, (slab + 1) * LANES)
        placed = place_heads(raw[:, at], gain_q[...], cosines[...], sines[...])
        query[:, at] = (placed.astype(BF).astype(F32) * 0.125).astype(BF)


def attend_kernel(tile, seq, spots, seg_row, query, w_out, *refs):
    pieces = refs[:-10]
    moved, *sums = refs[-10:-5]
    mixed, ext, low, total, seg = refs[-5:]
    rows = query.shape[0]
    heads = query.shape[1] // HEAD
    group = heads // 2
    me = spots[4]
    first_doc = spots[5 + seq]
    wide_row = jnp.broadcast_to(seg_row[...].astype(F32), (LANES, rows))
    seg[...] = wide_row.T[:, :1].astype(jnp.int32)
    lane = lane_of((rows, LANES))
    for head in range(heads):
        low[head] = jnp.where(lane < HEAD, low_head(query, head), 0.0).astype(BF)
    total[...] = jnp.zeros_like(total)

    def tile_step(back, block, piece):
        start = (me - back) * rows + block * tile

        @pl.when(start + tile > first_doc)
        def _():
            kv = piece[pl.ds(block * tile, tile), :]
            shape = (rows, tile)
            place = start + lax.broadcasted_iota(jnp.int32, shape, 1)
            allowed = place >= seg[...]
            if back == 0:
                allowed &= place <= me * rows + lax.broadcasted_iota(jnp.int32, shape, 0)
            for which in range(2):
                key = with_ones(kv[:, :LANES], which).astype(BF)
                value = with_ones(kv[:, LANES:], which).astype(BF)
                for head in range(which * group, (which + 1) * group):
                    scores = jnp.where(allowed, nt_dot(low[head], key), -1e30)
                    total[head] += nn_dot(jnp.exp(scores).astype(BF), value)

    for back, piece in enumerate(pieces):

        @pl.when(me >= back)
        def _(back=back, piece=piece):
            def step(block, carry):
                tile_step(back, block, piece)
                return carry

            lax.fori_loop(0, rows // tile, step, 0)

    for slab in range(heads // 2):
        parts = []
        for head in (2 * slab, 2 * slab + 1):
            got = total[head]
            weight = got[:, HEAD : HEAD + 1]
            parts.append(got / weight)
            ext[head] = with_minus(low[head].astype(F32), jnp.log(weight))
        joined = jnp.where(lane < HEAD, parts[0], pltpu.roll(parts[1], HEAD, 1))
        mixed[:, slab * LANES : (slab + 1) * LANES] = joined.astype(BF)
    block = rows // 4
    for i, at in enumerate(spots_of(spots, 4, rows)):
        moved[i * block : (i + 1) * block, :] = mixed[at, :]
    split_rows(nn_dot(moved[...], w_out[...]), *sums)


def attend_back_kernel(
    tile,
    count,
    seq,
    spots,
    seg,
    ext,
    mixed,
    own,
    near,
    far,
    far_near,
    w_out,
    q_raw,
    cosines,
    sines,
    gain_q,
    *refs,
):
    pieces = refs[:count]
    d_rows, d_q_raw, gain_part = refs[count : count + 3]
    d_pieces = refs[count + 3 : 2 * count + 3]
    d_ext, d_query, d_mixed = refs[2 * count + 3 :]
    rows = mixed.shape[0]
    heads = mixed.shape[1] // HEAD
    group = heads // 2
    me = spots[4]
    first_doc = spots[5 + seq]
    lane = lane_of((rows, LANES))
    block = rows // 4
    for i, part in enumerate((own, near, far, far_near)):
        d_rows[i * block : (i + 1) * block, :] = part[...]
    moved = nt_dot(d_rows[...], w_out[...]).astype(BF)
    for i, at in enumerate(spots_of(spots, 4, rows)):
        d_mixed[at, :] = moved[i * block : (i + 1) * block]
    for head in range(heads):
        grad = jnp.where(lane < HEAD, low_head(d_mixed, head), 0.0)
        delta = jnp.sum(grad * low_head(mixed, head), axis=-1, keepdims=True)
        d_ext[head] = with_minus(grad, delta)
    d_query[...] = jnp.zeros_like(d_query)
    low_tile = lane_of((tile, LANES)) < HEAD

    def tile_step(back, block, piece, d_piece):
        start = (me - back) * rows + block * tile
        needed = start + tile > first_doc
        at = pl.ds(block * tile, tile)

        @pl.when(needed)
        def _():
            kv = piece[at, :]
            shape = (tile, rows)
            place = start + lax.broadcasted_iota(jnp.int32, shape, 0)
            allowed = place >= seg[...]
            if back == 0:
                allowed &= place <= me * rows + lax.broadcasted_iota(jnp.int32, shape, 1)
            d_keys = []
            d_values = []
            for which in range(2):
                key_f = with_ones(kv[:, :LANES], which)
                key = key_f.astype(BF)
                key_t = key_f.T[:HEAD].astype(BF)
                value = with_ones(kv[:, LANES:], which).astype(BF)
                d_key = jnp.zeros((tile, LANES), F32)
                d_value = jnp.zeros((tile, LANES), F32)
                for head in range(which * group, (which + 1) * group):
                    scores = jnp.where(allowed, nt_dot(key, ext[head]), -1e30)
                    probs = jnp.exp(scores)
                    d_scores = (probs * nt_dot(value, d_ext[head])).astype(BF)
                    d_value += nn_dot(probs.astype(BF), d_ext[head])
                    d_key += nn_dot(d_scores, ext[head])
                    d_query[head * HEAD : (head + 1) * HEAD, :] += nn_dot(key_t, d_scores)
                d_keys.append(d_key)
                d_values.append(d_value)
            for spot, pair in enumerate((d_keys, d_values)):
                joined = jnp.where(low_tile, pair[0], pltpu.roll(pair[1], HEAD, 1))
                d_piece[at, spot * LANES : (spot + 1) * LANES] = joined.astype(BF)

        @pl.when(jnp.logical_not(needed))
        def _():
            d_piece[at, :] = jnp.zeros((tile, 2 * LANES), BF)

    for back, (piece, d_piece) in enumerate(zip(pieces, d_pieces)):

        @pl.when(me >= back)
        def _(back=back, piece=piece, d_piece=d_piece):
            def step(block, carry):
                tile_step(back, block, piece, d_piece)
                return carry

            lax.fori_loop(0, rows // tile, step, 0)

        @pl.when(me < back)
        def _(d_piece=d_piece):
            d_piece[...] = jnp.zeros_like(d_piece)

    for slab in range(heads // 2):
        at = slice(slab * LANES, (slab + 1) * LANES)
        grad = (d_query[at, :].T * 0.125).astype(BF).astype(F32)
        out, part = rope_norm_back(grad, q_raw[:, at], cosines[...], sines[...], gain_q[...])
        d_q_raw[:, at] = out
        gain_part[:, at] = part


def rope_norm_back(grad, raw, cosines, sines, gains):
    back = turn(grad, cosines, -sines)
    scale = lax.rsqrt(head_mean(raw * raw) + EPS)
    unit = raw * scale
    scaled = back * gains
    out = scale * (scaled - unit * head_mean(scaled * unit))
    part = jnp.sum(back * unit, axis=0, keepdims=True)
    return out.astype(BF), part


def key_back_kernel(
    quarters,
    d_piece,
    got,
    d_q_raw,
    k_raw,
    cosines,
    sines,
    gain_k,
    w_query,
    w_key,
    w_value,
    d_qkv,
    own,
    near,
    far,
    far_near,
    gain_part,
    moved,
):
    q_cols = d_q_raw.shape[1]
    total = (d_piece[...].astype(F32) + got[...].astype(F32)).astype(BF)
    d_key = total[:, :LANES].astype(F32)
    out, part = rope_norm_back(d_key, k_raw[...], cosines[...], sines[...], gain_k[...])
    gain_part[...] = part
    d_qkv[:, :q_cols] = d_q_raw[...]
    d_qkv[:, q_cols : q_cols + LANES] = out
    d_qkv[:, q_cols + LANES :] = total[:, LANES:]
    block = moved.shape[0] // 4
    for i, at in enumerate(spots_of(quarters, 4, moved.shape[0])):
        moved[i * block : (i + 1) * block, :] = d_qkv[at, :]
    grad = nt_dot(moved[:, :q_cols], w_query[...])
    grad += nt_dot(moved[:, q_cols : q_cols + LANES], w_key[...])
    grad += nt_dot(moved[:, q_cols + LANES :], w_value[...])
    split_rows(grad, own, near, far, far_near)


def spots_of(spots, count, rows, skip=0):
    block = rows // count
    return [pl.ds(pl.multiple_of(spots[skip + i] * block, 16), block) for i in range(count)]


def split_rows(total, *parts):
    block = total.shape[0] // len(parts)
    for i, part in enumerate(parts):
        part[...] = total[i * block : (i + 1) * block].astype(part.dtype)


def d_active_kernel(quarters, rows, right, moved, out):
    @pl.when(pl.program_id(0) == 0)
    def _():
        block = rows.shape[0] // 4
        for i, at in enumerate(spots_of(quarters, 4, rows.shape[0])):
            moved[i * block : (i + 1) * block, :] = rows[at, :]

    out[...] = nt_dot(moved[...], right[...]).astype(BF)


def units_kernel(
    units, own, near, far, far_near, gate_t, up_t, d_active, rows, active, d_gate, d_upper
):
    @pl.when(pl.program_id(0) == 0)
    def _():
        block = own.shape[0]
        for i, part in enumerate((own, near, far, far_near)):
            rows[i * block : (i + 1) * block, :] = part[...]

    x = rows[...]
    wide = active.shape[1]
    half = wide // 2
    for part in range(2):
        at = slice(part * half, (part + 1) * half)
        gate = nt_dot(x, gate_t[at, :])
        upper = nt_dot(x, up_t[at, :])
        column = pl.program_id(0) * wide + part * half + lane_of(gate.shape)
        real = column < units
        sigma = jax.nn.sigmoid(gate)
        silu = gate * sigma
        grad = d_active[:, at].astype(F32)
        active[:, at] = jnp.where(real, silu * upper, 0.0).astype(BF)
        d_upper[:, at] = jnp.where(real, grad * silu, 0.0).astype(BF)
        slope = grad * upper * (sigma + silu * (1.0 - sigma))
        d_gate[:, at] = jnp.where(real, slope, 0.0).astype(BF)


def columns_kernel(count, *refs):
    depth = refs[count].shape[0]
    total = sum(nn_dot(refs[i][:, :depth], refs[count + i][...]) for i in range(count))
    split_rows(total, *refs[2 * count :])


def masked_sum(valid, values):
    mask = jnp.broadcast_to(valid[0].astype(F32), (8, values.shape[0]))
    total = lax.dot_general(
        mask,
        values,
        (((1,), (0,)), ((), ())),
        precision=lax.Precision.HIGHEST,
        preferred_element_type=F32,
    )
    return total[:1]


def pass_back_kernel(first, second, *refs):
    out = refs[-1]
    local = first.shape[0]
    for i, part in enumerate((first, second)):
        at = slice(i * local, (i + 1) * local)
        if len(refs) > 1:
            out[at, :] = (part[...].astype(F32) + refs[0][at, :].astype(F32)).astype(BF)
        else:
            out[at, :] = part[...]


def norm_two_kernel(spot, kept, got_far, got, hidden, valid, gain, normed, middle, squares):
    attn = kept[...] + got_far[...].astype(F32) + got[...].astype(F32)
    before = hidden[...].astype(F32)
    total = before + attn
    middle[...] = total
    normed[...] = (total * rms_scale(total) * gain[...]).astype(BF)
    squares[0:1, :] = masked_sum(valid, attn * attn)
    squares[1:2, :] = masked_sum(valid, before * before)


def middle_back_kernel(spot, kept, got_far, got, middle, cot, gain, d_low, d_middle, gain_part):
    grad = kept[...] + got_far[...].astype(F32) + got[...].astype(F32)
    before = middle[...]
    scale = rms_scale(before)
    unit = before * scale
    gain_part[...] = jnp.sum(grad * unit, axis=0, keepdims=True)
    total = cot[...].astype(F32) + norm_back(grad, unit, scale, gain[...])
    d_middle[...] = total
    d_low[...] = total.astype(BF)


def hidden_back_kernel(spot, kept, got_far, got, hidden, d_middle, gain, out, gain_part):
    grad = kept[...] + got_far[...].astype(F32) + got[...].astype(F32)
    before = hidden[...].astype(F32)
    scale = rms_scale(before)
    unit = before * scale
    gain_part[...] = jnp.sum(grad * unit, axis=0, keepdims=True)
    out[...] = (d_middle[...] + norm_back(grad, unit, scale, gain[...])).astype(BF)


def output_kernel(spot, kept, got_far, got, middle, valid, out, squares):
    branch = kept[...] + got_far[...].astype(F32) + got[...].astype(F32)
    out[...] = (middle[...] + branch).astype(BF)
    squares[...] = masked_sum(valid, branch * branch)


def place_kernel(quarters, *refs):
    parts, out = refs[:-1], refs[-1]
    block = parts[0].shape[0]
    for i, part in enumerate(parts):
        first = pl.multiple_of((i // 4 * 4 + quarters[i % 4]) * block, 16)
        out[pl.ds(first, block), :] = part[...]


def rope_tables(length):
    places = np.arange(length).astype(np.float32)
    half = HEAD // 2
    freqs = np.float32(THETA) ** (-np.arange(half).astype(np.float32) / np.float32(half))
    angles = (places[:, None] * freqs.astype(np.float32)[None, :]).astype(np.float64)
    cosines = np.cos(angles).astype(np.float32)
    sines = np.sin(angles).astype(np.float32)
    return (
        np.concatenate([cosines] * 4, axis=1),
        np.concatenate([-sines, sines, -sines, sines], axis=1),
    )


def after(value, *others):
    return lax.optimization_barrier((value,) + others)[0]


def params():
    return pltpu.CompilerParams(vmem_limit_bytes=VMEM_LIMIT)


def call(kernel, name, **kw):
    small = pl.CostEstimate(flops=1, bytes_accessed=1, transcendentals=0)
    return pl.pallas_call(kernel, compiler_params=params(), cost_estimate=small, name=name, **kw)


def shape(*dims, dtype=BF):
    return jax.ShapeDtypeStruct(dims, dtype)


def fixed(*dims):
    return pl.BlockSpec(dims, lambda i: (0,) * len(dims))


def by_row(rows, cols, first=0):
    return pl.BlockSpec((rows, cols), lambda i: (first + i, 0))


def by_block(rows, cols, spot):
    return pl.BlockSpec((rows, cols), lambda i: (spot, 0))


def by_col(rows, cols):
    return pl.BlockSpec((rows, cols), lambda i: (0, i))


SMEM = pl.BlockSpec(memory_space=pltpu.SMEM)
UNITS = 512
WIDE_UNITS = 896
PAD = 256


def flip(n, bit):
    return [(i, i ^ bit) for i in range(n)]


def cut(array, start, size):
    return lax.dynamic_slice_in_dim(array, start, size, axis=0)


class Order:
    def __init__(self):
        self.last = None

    def tie(self, *values):
        if self.last is not None:
            values = lax.optimization_barrier(values + (self.last,))[:-1]
        return values

    def mark(self, value):
        self.last = value
        return value

    def wait(self, values, spot):
        values[spot] = self.mark(self.tie(values[spot])[0])


def build(mesh):
    dp_n, ctx_n, tp_n = (mesh.shape[a] for a in ("dp", "ctx", "tp"))
    blocks = dp_n * ctx_n

    def bits(axis, n):
        out = []
        while n > 1:
            n //= 2
            out.append((axis, n))
        return out

    steps = bits("dp", dp_n) + bits("ctx", ctx_n)[::-1]
    sizes = {"dp": dp_n, "ctx": ctx_n, "tp": tp_n}

    def swap(value, step):
        axis, bit = step
        return lax.ppermute(value, axis, flip(sizes[axis], bit))

    core, across = ("tp", 1), ("tp", 2)

    def bit_of(step):
        axis, bit = step
        return lax.axis_index(axis) // bit % 2

    def halves(part, step, outer):
        axis, bit = step
        left = 1 if axis == "dp" else outer * ctx_n // (2 * bit)
        view = part.reshape(left, 2, -1, part.shape[-1])
        mine = bit_of(step)
        pick = lambda which: lax.dynamic_index_in_dim(view, which, 1, keepdims=False).reshape(
            -1, part.shape[-1]
        )
        return pick(mine), pick(1 - mine)

    def body(
        hidden,
        cotangent,
        segments,
        valid,
        w_query,
        w_key,
        w_value,
        w_out,
        w_gate,
        w_up,
        w_down,
        gain_attn,
        gain_ffn,
        gain_query,
        gain_key,
    ):
        seqs, local, width = hidden.shape
        rows = seqs * local
        every = range(seqs)
        q_cols = w_query.shape[1]
        units = w_gate.shape[1]
        wide = pl.cdiv(units, PAD) * PAD
        heads = q_cols // HEAD
        me = lax.axis_index("ctx")
        member = lax.axis_index("tp")
        o = Order()
        cosines, sines = (jnp.asarray(t) for t in rope_tables(local * ctx_n))
        hidden_r = hidden.reshape(rows, width)
        cot_r = cotangent.reshape(rows, width)
        valid_r = valid.reshape(seqs * 4, 1, local // 4)
        gate_t, up_t = w_gate.T, w_up.T
        gq = jnp.concatenate([gain_query, gain_query])[None]
        gk = jnp.concatenate([gain_key, gain_key])[None]
        gain_a, gain_f = gain_attn[None], gain_ffn[None]
        tile = 256
        half, quarter = local // 2, local // 4
        own = (member % 2) * 2 + member // 2
        spots = jnp.stack([own ^ i for i in range(4)] + [me])
        spots = jnp.concatenate([spots, segments[:, 0]]).astype(jnp.int32)
        seg_rows = [segments[s][None] for s in every]
        _, *seg_rows = lax.optimization_barrier((spots, *seg_rows))

        def stage(kernel, name, args, outs, grid=1, scratch=(), placed=False, shared=None):
            arrays = [a for a, _ in args]
            arrays[:1] = o.tie(arrays[0])
            fix = lambda spec: pl.BlockSpec(spec.block_shape, lambda i, *s: spec.index_map(i))
            of = lambda spec: spec.spec if isinstance(spec, Dynamic) else fix(spec)
            specs = [of(spec) for _, spec in args]
            old = list(shared or [])
            count = int(placed) + len(args)
            run = kernel
            if old:
                run = lambda *refs: kernel(*refs[:count], *refs[count + len(old) :])
            got = pl.pallas_call(
                run,
                grid_spec=pltpu.PrefetchScalarGridSpec(
                    num_scalar_prefetch=int(placed),
                    grid=(grid,),
                    in_specs=specs + [pl.BlockSpec(memory_space=pl.ANY)] * len(old),
                    out_specs=[fix(s) for _, s in outs],
                    scratch_shapes=list(scratch),
                ),
                out_shape=[s for s, _ in outs],
                input_output_aliases={count + i: i for i in range(len(old))},
                compiler_params=params(),
                cost_estimate=pl.CostEstimate(flops=1, bytes_accessed=1, transcendentals=0),
                name=name,
            )(*([spots] if placed else []), *arrays, *old)
            o.mark(got[0])
            return got

        class Dynamic:
            def __init__(self, cols, seq):
                self.spec = pl.BlockSpec((quarter, cols), lambda i, s: (seq * 4 + s[0], 0))

        def full(array):
            return (array, fixed(*array.shape))

        def fulls(arrays):
            return [full(a) for a in arrays]

        def new(*dims, dtype=BF):
            return (shape(*dims, dtype=dtype), fixed(*dims))

        def part(cols, s):
            return by_block(local, cols, s)

        class Table(Dynamic):
            def __init__(self, rows):
                per = local // rows
                self.spec = pl.BlockSpec((rows, LANES), lambda i, s: (s[4] * per + i, 0))

        class Valid(Dynamic):
            def __init__(self, seq):
                self.spec = pl.BlockSpec((1, 1, quarter), lambda i, s: (seq * 4 + s[0], 0, 0))

        tables = lambda n: [(t, Table(n)) for t in (cosines, sines)]

        parts_out = [
            (shape(quarter, width, dtype=d), fixed(quarter, width)) for d in (F32, F32, BF, BF)
        ]

        def split_columns(which, lefts, rights, name):
            count = len(lefts)
            depth, cols = rights[0].shape
            tokens = local * len(which)
            outs = stage(
                functools.partial(columns_kernel, count),
                name,
                [(l, by_block(tokens, l.shape[1], which[0] // len(which))) for l in lefts]
                + [(r, by_col(depth, UNITS)) for r in rights],
                [(out, by_col(quarter, UNITS)) for out, _ in parts_out] * len(which),
                grid=cols // UNITS,
            )
            return [outs[i * 4 : i * 4 + 4] for i in range(len(which))]

        class Spread:
            def __init__(self, own, near, far, far_near):
                self.own, self.near = own, near
                self.far = [far_near, far]

            def first(self):
                self.far = list(o.tie(*self.far))
                o.mark(self.far[0])
                self.got = [swap(f, core) for f in self.far]

            def second(self):
                near, got = o.tie(self.near, self.got[0])
                away = o.mark((near + got.astype(F32)).astype(BF))
                self.got[0] = swap(away, across)

            def parts(self):
                return fulls([self.own, self.got[1], self.got[0]])

        class Collect:
            def __init__(self, mine):
                self.got = [mine, swap(mine, across)]

            def second(self):
                o.wait(self.got, 1)
                self.got += [swap(value, core) for value in self.got]

        half_of = lambda left, which: lax.dynamic_slice_in_dim(
            left, which * (width // 2), width // 2, axis=1
        )

        def other_ctx(left, which):
            view = left.reshape(rows, blocks // 2, 2, width // blocks)
            return lax.dynamic_index_in_dim(view, which, 2, keepdims=False).reshape(rows, -1)

        class Grad:
            def __init__(self, *pairs, ctx_first=False):
                dp_bits = [step for step in steps if step[0] == "dp"]
                ctx_bits = [step for step in steps if step[0] == "ctx"]
                self.steps = ctx_bits + dp_bits if ctx_first else dp_bits + ctx_bits
                self.outer = dp_n if ctx_first else 1
                pick = other_ctx if ctx_first else half_of
                bit = bit_of(self.steps[0])
                self.rights = [right for _, right in pairs]
                self.keep = [lambda left=left: pick(left, bit) for left, _ in pairs]
                self.give = [lambda left=left: pick(left, 1 - bit) for left, _ in pairs]

            def away(self):
                rights = o.tie(*self.rights)
                parts = [tn_dot(left(), r).astype(BF) for left, r in zip(self.give, rights)]
                self.out = o.mark(jnp.concatenate(parts, axis=1))

            def send(self, *waits):
                for grad in waits:
                    grad.wait()
                (out,) = o.tie(self.out)
                self.got = swap(o.mark(out), self.steps[0])
                self.left_steps = self.steps[1:]

            def wait(self):
                (self.got,) = o.tie(self.got)
                o.mark(self.got)

            def columns(self, got):
                ends = np.cumsum([r.shape[1] for r in self.rights])
                return [got[:, e - r.shape[1] : e] for r, e in zip(self.rights, ends)]

            def own(self):
                *rights, got = o.tie(*self.rights, self.got)
                self.terms = []
                for left, r, g in zip(self.keep, rights, self.columns(got)):
                    self.terms.append([o.mark(tn_dot(left(), r) + g.astype(F32))])
                self.pass_on()

            def pass_on(self):
                if not self.left_steps:
                    return
                step = self.left_steps.pop(0)
                stay, away = [], []
                for terms in self.terms:
                    pairs = [halves(t, step, self.outer) for t in terms]
                    stay.append([p[0] for p in pairs])
                    away.append(sum(p[1].astype(F32) for p in pairs).astype(BF))
                got = swap(o.mark(jnp.concatenate(away, axis=1)), step)
                self.terms = [t + [g] for t, g in zip(stay, self.columns(got))]

            def arrive(self):
                for terms in self.terms:
                    (terms[-1],) = o.tie(terms[-1])

            def third(self):
                self.arrive()
                self.pass_on()

            def last(self):
                while self.left_steps:
                    self.third()
                self.arrive()
                return [o.mark(sum(t.astype(F32) for t in terms)) for terms in self.terms]

        up = lambda hops: [(i, i + hops) for i in range(ctx_n - hops)]
        down = [(i + 1, i) for i in range(ctx_n - 1)]
        normed, k_raw, pieces = None, [], []
        step = 256
        per = local // step

        class Around(Dynamic):
            def __init__(self):
                self.spec = pl.BlockSpec((step, LANES), lambda i, s: (s[4] * per + i % per, 0))

        for s in every:
            normed, sent, raw = stage(
                key_value_kernel,
                "key_value",
                [(hidden_r, by_row(step, width, s * per))]
                + fulls([gain_a, w_key, w_value])
                + tables(step)
                + fulls([gk]),
                [
                    (shape(rows, width), by_row(step, width, s * per)),
                    (shape(local, 2 * LANES), by_row(step, 2 * LANES)),
                    (shape(local, LANES, dtype=F32), by_row(step, LANES)),
                ],
                grid=per,
                placed=True,
                shared=[normed] if s else None,
            )
            k_raw.append(raw)
            pieces.append([sent])

        def send_keys(s, direct):
            for hops in range(1, ctx_n if direct else min(3, ctx_n)):
                pieces[s].append(lax.ppermute(pieces[s][0], "ctx", up(hops)))

        for s in every:
            send_keys(s, True)
        query, q_raw = stage(
            query_kernel,
            "query",
            [(normed, by_row(step, width)), full(w_query)]
            + [(t, Around()) for t in (cosines, sines)]
            + fulls([gq]),
            [(shape(rows, q_cols, dtype=d), by_row(step, q_cols)) for d in (BF, F32)],
            grid=seqs * per,
            placed=True,
        )
        d_active, cot_moved = [], None

        def d_active_of(s):
            nonlocal cot_moved
            cot_moved, grad = stage(
                d_active_kernel,
                "d_active",
                [(cot_r, part(width, s)), (w_down, by_row(WIDE_UNITS, width))],
                [
                    (shape(rows, width), part(width, s)),
                    (shape(local, wide), by_col(local, WIDE_UNITS)),
                ],
                grid=pl.cdiv(wide, WIDE_UNITS),
                placed=True,
                shared=[cot_moved] if s else None,
            )
            d_active.append(grad)

        d_active_of(0)
        for s in every[1:]:
            d_active_of(s)

        mixed, mixed_moved, exts, attn = [], None, [], []

        def attend(s):
            nonlocal mixed_moved
            mixed_moved, *parts, mix, ext = stage(
                functools.partial(attend_kernel, tile, s),
                "attend",
                [full(seg_rows[s]), (query, part(q_cols, s))] + fulls([w_out] + pieces[s]),
                [(shape(rows, q_cols), part(q_cols, s))]
                + parts_out
                + [new(local, q_cols), new(heads, local, LANES)],
                scratch=[
                    pltpu.VMEM((heads, local, LANES), BF),
                    pltpu.VMEM((heads, local, LANES), F32),
                    pltpu.VMEM((local, 1), jnp.int32),
                ],
                placed=True,
                shared=[mixed_moved] if s else None,
            )
            mixed.append(mix)
            exts.append(ext)
            attn.append(Spread(*parts))

        middle, squares, two = [], [], []

        def norm_two(s):
            normed_own, mid, square = stage(
                norm_two_kernel,
                "norm_two",
                attn[s].parts()
                + [(hidden_r, Dynamic(width, s)), (valid_r, Valid(s)), full(gain_f)],
                [new(quarter, width), new(quarter, width, dtype=F32), new(2, width, dtype=F32)],
                placed=True,
            )
            middle.append(mid)
            squares.append(square)
            two.append(Collect(normed_own))

        two_rows = active = d_gate = d_upper = None

        def units_of(s):
            nonlocal two_rows, active, d_gate, d_upper
            outs = (two_rows, active, d_gate, d_upper)
            two_rows, active, d_gate, d_upper = stage(
                functools.partial(units_kernel, units),
                "units",
                fulls(two[s].got)
                + [(gate_t, by_row(UNITS, width)), (up_t, by_row(UNITS, width))]
                + [(d_active[s], by_col(local, UNITS))],
                [(shape(rows, width), part(width, s))]
                + [(shape(rows, wide), pl.BlockSpec((local, UNITS), lambda i: (s, i)))] * 3,
                grid=pl.cdiv(wide, UNITS),
                shared=outs if s else None,
            )

        for s in every:
            attend(s)
        for s in every:
            attn[s].first()
        for s in every:
            attn[s].second()
        for s in every:
            norm_two(s)
        for s in every:
            two[s].second()
            units_of(s)

        down_sum = Grad((cot_moved, active))
        gate_sum = Grad((two_rows, d_gate))
        up_sum = Grad((two_rows, d_upper))
        down_sum.away()
        down_sum.send()
        d_two = [
            Spread(*parts)
            for parts in split_columns(every, [d_gate, d_upper], [gate_t, up_t], "d_two")
        ]
        for s in every:
            d_two[s].first()
        for s in every:
            d_two[s].second()

        branch, out_squares, out_parts = [], [], []

        def branch_of(s):
            branch.append(Spread(*split_columns([s], [active], [w_down], "branch")[0]))

        def output_of(s):
            value, square = stage(
                output_kernel,
                "output",
                branch[s].parts() + [full(middle[s]), (valid_r, Valid(s))],
                [new(quarter, width), new(1, width, dtype=F32)],
                placed=True,
            )
            out_squares.append(square)
            out_parts.append(Collect(value))

        d_middle, d_low, gain_f_parts = [], [], []

        def middle_back(s):
            low, mid, gains = stage(
                middle_back_kernel,
                "middle_back",
                d_two[s].parts() + [full(middle[s]), (cot_r, Dynamic(width, s)), full(gain_f)],
                [new(quarter, width), new(quarter, width, dtype=F32), new(1, width, dtype=F32)],
                placed=True,
            )
            d_middle.append(mid)
            gain_f_parts.append(gains)
            d_low.append(Collect(low))

        branch_of(0)
        for s in every:
            middle_back(s)
        for s in every[1:]:
            branch_of(s)
        d_low[0].second()
        gate_sum.away()
        down_sum.wait()
        up_sum.away()
        gate_sum.send()
        down_sum.own()
        for s in every[1:]:
            d_low[s].second()
        for s in every:
            branch[s].first()

        d_q_raw, d_pieces, d_rows, passed = [], [], None, None
        gain_q_parts = []

        def attend_back(s):
            nonlocal d_rows
            outs = stage(
                functools.partial(attend_back_kernel, tile, ctx_n, s),
                "attend_back",
                fulls([seg_rows[s], exts[s], mixed[s]] + d_low[s].got + [w_out])
                + [(q_raw, part(q_cols, s))]
                + tables(local)
                + fulls([gq] + pieces[s]),
                [
                    (shape(rows, width), part(width, s)),
                    new(local, q_cols),
                    new(1, q_cols, dtype=F32),
                ]
                + [new(local, 2 * LANES)] * ctx_n,
                scratch=[
                    pltpu.VMEM((heads, local, LANES), BF),
                    pltpu.VMEM((q_cols, local), F32),
                    pltpu.VMEM((local, q_cols), BF),
                ],
                placed=True,
                shared=[d_rows] if s else None,
            )
            d_rows = outs[0]
            d_q_raw.append(outs[1])
            gain_q_parts.append(outs[2])
            d_pieces.append(outs[3:])

        def pass_back(back):
            nonlocal passed
            mine = [d_pieces[s][back] for s in every]
            args = fulls(mine)
            if back < ctx_n - 1:
                args.append(full(passed))
            passed = stage(pass_back_kernel, "pass_back", args, [new(rows, 2 * LANES)])[0]
            passed = lax.ppermute(passed, "ctx", down)

        d_qkv, d_one, gain_k_parts = None, [], []

        def key_back(s):
            nonlocal d_qkv
            d_qkv, *parts, gains = stage(
                key_back_kernel,
                "key_back",
                [
                    full(d_pieces[s][0]),
                    (passed, by_block(local, 2 * LANES, s)),
                    full(d_q_raw[s]),
                    full(k_raw[s]),
                ]
                + tables(local)
                + fulls([gk, w_query, w_key, w_value]),
                [(shape(rows, q_cols + 2 * LANES), part(q_cols + 2 * LANES, s))]
                + parts_out
                + [new(1, LANES, dtype=F32)],
                scratch=[pltpu.VMEM((local, q_cols + 2 * LANES), BF)],
                placed=True,
                shared=[d_qkv] if s else None,
            )
            gain_k_parts.append(gains)
            d_one.append(Spread(*parts))

        gain_a_parts, back_hidden = [], []

        def hidden_back(s):
            grad, gains = stage(
                hidden_back_kernel,
                "hidden_back",
                d_one[s].parts()
                + [(hidden_r, Dynamic(width, s)), full(d_middle[s]), full(gain_a)],
                [new(quarter, width), new(1, width, dtype=F32)],
                placed=True,
            )
            gain_a_parts.append(gains)
            back_hidden.append(Collect(grad))

        def place(parts):
            return stage(
                place_kernel,
                "place",
                fulls([p for c in parts for p in c.got]),
                [new(rows, width)],
                placed=True,
            )[0]

        attend_back(0)
        for s in every:
            branch[s].second()
        down_sum.third()
        for s in every[1:]:
            attend_back(s)
        up_sum.send(gate_sum)
        if ctx_n > 1:
            pass_back(ctx_n - 1)
        (grad_down,) = down_sum.last()
        for i, back in enumerate(range(ctx_n - 2, 0, -1)):
            pass_back(back)
            if i == 0:
                for s in every:
                    output_of(s)
        gate_sum.own()
        for s in every:
            out_parts[s].second()
        for s in every:
            key_back(s)
        for s in every:
            d_one[s].first()
        rest_sum = Grad((normed, d_qkv), (d_rows, mixed_moved))
        rest_sum.away()
        rest_sum.send(up_sum)
        for s in every:
            d_one[s].second()
        up_sum.own()
        gate_sum.third()
        output = place(out_parts).reshape(seqs, local, width)
        for s in every:
            hidden_back(s)
        rest_sum.wait()
        rest_sum.own()
        for s in every:
            back_hidden[s].second()
        (grad_gate,) = gate_sum.last()

        gain_q_part = sum(gain_q_parts).reshape(heads, HEAD).sum(axis=0)
        gain_k_part = sum(gain_k_parts).reshape(2, HEAD).sum(axis=0)
        total_square = sum(squares).sum(axis=1)
        branch_square = sum(out_squares).sum()
        count = jnp.sum(valid).astype(F32) / tp_n
        small = jnp.concatenate(
            [
                sum(gain_a_parts)[0],
                sum(gain_f_parts)[0],
                gain_q_part,
                gain_k_part,
                jnp.stack([total_square[1], total_square[0], branch_square, count]),
                jnp.zeros((LANES - 4,), F32),
            ]
        ).reshape(-1, LANES)
        (small,) = o.tie(small)
        flips = [(a, b) for a in ("tp", "dp", "ctx") for _, b in bits(a, sizes[a])[::-1]]

        def sum_step():
            nonlocal small
            small, got = o.tie(small, swap(small, flips.pop(0)))
            small = o.mark(small + got)

        ctx_flips = sum(1 for axis, _ in flips if axis == "ctx")
        while len(flips) > ctx_flips:
            sum_step()
        up_sum.third()
        grad_hidden = place(back_hidden).reshape(seqs, local, width)
        while len(flips) > 1:
            sum_step()
        rest_sum.third()
        (grad_up,) = up_sum.last()
        while flips:
            sum_step()
        grad_qkv, grad_out = rest_sum.last()
        grad_down, grad_gate, grad_up = (g[:, :units] for g in (grad_down, grad_gate, grad_up))
        grad_down, grad_out = grad_down.T, grad_out.T

        small = small.reshape(-1)
        at = 2 * width + 2 * HEAD
        denom = jnp.maximum(small[at + 3], 1.0) * width
        root = lambda spot: jnp.sqrt(small[at + spot] / denom)
        return (
            output,
            grad_hidden,
            grad_qkv[:, :q_cols],
            grad_qkv[:, q_cols : q_cols + LANES],
            grad_qkv[:, q_cols + LANES :],
            grad_out,
            grad_gate,
            grad_up,
            grad_down,
            small[:width],
            small[width : 2 * width],
            small[2 * width : 2 * width + HEAD],
            small[2 * width + HEAD : at],
            root(0),
            root(1),
            root(2),
        )

    return body


def solution(mesh):
    tokens = P("dp", "ctx", None)
    marks = P("dp", "ctx")
    columns = P(None, "tp")
    rows = P("tp", None)
    by_rows = P(("dp", "ctx"), "tp")
    by_columns = P("tp", ("dp", "ctx"))
    in_specs = (tokens, tokens, marks, marks, columns, columns, columns, rows)
    in_specs += (columns, columns, rows, P(), P(), P(), P())
    out_specs = (tokens, tokens, by_rows, by_rows, by_rows, by_columns, by_rows, by_rows)
    out_specs += (by_columns, P(), P(), P(), P(), P(), P(), P())
    return jax.shard_map(
        build(mesh), mesh=mesh, in_specs=in_specs, out_specs=out_specs, check_vma=False
    )
```

```python
import functools

import jax
import jax.numpy as jnp
import numpy as np
from jax import lax
from jax.experimental import pallas as pl
from jax.experimental.pallas import tpu as pltpu
from jax.sharding import PartitionSpec as P

HEAD = 64
EPS = 1e-05
THETA = 1000000.0
BF = jnp.bfloat16
F32 = jnp.float32
LANES = 128
VMEM_LIMIT = 56 * 1024 * 1024


def nn_dot(left, right):
    return lax.dot_general(left, right, (((1,), (0,)), ((), ())), preferred_element_type=F32)


def nt_dot(left, right):
    return lax.dot_general(left, right, (((1,), (1,)), ((), ())), preferred_element_type=F32)


def tn_dot(left, right):
    return lax.dot_general(left, right, (((0,), (0,)), ((), ())), preferred_element_type=F32)


def rms_scale(values):
    return lax.rsqrt(jnp.mean(values * values, axis=-1, keepdims=True) + EPS)


def norm_back(grads, unit, scale, gain):
    scaled = grads * gain
    return scale * (scaled - unit * jnp.mean(scaled * unit, axis=-1, keepdims=True))


def lane_of(shape):
    return lax.broadcasted_iota(jnp.int32, shape, len(shape) - 1)


def head_mean(slab):
    row = lax.broadcasted_iota(jnp.int32, (LANES, LANES), 0)
    col = lax.broadcasted_iota(jnp.int32, (LANES, LANES), 1)
    same = jnp.where((row < HEAD) == (col < HEAD), 1.0 / HEAD, 0.0).astype(BF)
    high = slab.astype(BF)
    rest = slab - high.astype(F32)
    mid = rest.astype(BF)
    low = (rest - mid.astype(F32)).astype(BF)
    return nn_dot(high, same) + nn_dot(mid, same) + nn_dot(low, same)


def turn(slab, cosines, sines):
    half = HEAD // 2
    lane = lane_of(slab.shape)
    partner = jnp.where(
        (lane & (HEAD - 1)) < half,
        pltpu.roll(slab, LANES - half, 1),
        pltpu.roll(slab, half, 1),
    )
    return slab * cosines + partner * sines


def with_ones(slab, which):
    wide = slab.astype(F32)
    if which == 1:
        wide = pltpu.roll(wide, HEAD, 1)
    lane = lane_of(wide.shape)
    return jnp.where(lane < HEAD, wide, jnp.where(lane < HEAD + 3, 1.0, 0.0))


def with_minus(low, column):
    first = (-column).astype(BF).astype(F32)
    rest = -column - first
    second = rest.astype(BF).astype(F32)
    third = rest - second
    lane = lane_of(low.shape)
    tail = jnp.where(
        lane == HEAD,
        first,
        jnp.where(lane == HEAD + 1, second, jnp.where(lane == HEAD + 2, third, 0.0)),
    )
    return jnp.where(lane < HEAD, low, tail).astype(BF)


def low_head(ref, head):
    slab = ref[:, (head // 2) * LANES : (head // 2 + 1) * LANES].astype(F32)
    return pltpu.roll(slab, HEAD, 1) if head % 2 else slab


def place_heads(raw, gains, cosines, sines):
    return turn(raw * lax.rsqrt(head_mean(raw * raw) + EPS) * gains, cosines, sines)


def key_value_kernel(spots, hidden, gain, wk, wv, cosines, sines, gain_k, normed, kv, k_raw):
    x = hidden[...].astype(F32)
    rows = (x * rms_scale(x) * gain[...]).astype(BF)
    normed[...] = rows
    key = nn_dot(rows, wk[...])
    k_raw[...] = key
    kv[:, :LANES] = place_heads(key, gain_k[...], cosines[...], sines[...]).astype(BF)
    kv[:, LANES:] = nn_dot(rows, wv[...]).astype(BF)


def query_kernel(spots, normed, wq, cosines, sines, gain_q, query, q_raw):
    raw = nn_dot(normed[...], wq[...])
    q_raw[...] = raw
    for slab in range(raw.shape[1] // LANES):
        at = slice(slab * LANES, (slab + 1) * LANES)
        placed = place_heads(raw[:, at], gain_q[...], cosines[...], sines[...])
        query[:, at] = (placed.astype(BF).astype(F32) * 0.125).astype(BF)


def attend_kernel(tile, seq, spots, seg_row, query, w_out, *refs):
    pieces = refs[:-10]
    moved, *sums = refs[-10:-5]
    mixed, ext, low, total, seg = refs[-5:]
    rows = query.shape[0]
    heads = query.shape[1] // HEAD
    group = heads // 2
    me = spots[4]
    first_doc = spots[5 + seq]
    wide_row = jnp.broadcast_to(seg_row[...].astype(F32), (LANES, rows))
    seg[...] = wide_row.T[:, :1].astype(jnp.int32)
    lane = lane_of((rows, LANES))
    for head in range(heads):
        low[head] = jnp.where(lane < HEAD, low_head(query, head), 0.0).astype(BF)
    total[...] = jnp.zeros_like(total)

    def tile_step(back, block, piece):
        start = (me - back) * rows + block * tile

        @pl.when(start + tile > first_doc)
        def _():
            kv = piece[pl.ds(block * tile, tile), :]
            shape = (rows, tile)
            place = start + lax.broadcasted_iota(jnp.int32, shape, 1)
            allowed = place >= seg[...]
            if back == 0:
                allowed &= place <= me * rows + lax.broadcasted_iota(jnp.int32, shape, 0)
            for which in range(2):
                key = with_ones(kv[:, :LANES], which).astype(BF)
                value = with_ones(kv[:, LANES:], which).astype(BF)
                for head in range(which * group, (which + 1) * group):
                    scores = jnp.where(allowed, nt_dot(low[head], key), -1e30)
                    total[head] += nn_dot(jnp.exp(scores).astype(BF), value)

    for back, piece in enumerate(pieces):

        @pl.when(me >= back)
        def _(back=back, piece=piece):
            def step(block, carry):
                tile_step(back, block, piece)
                return carry

            lax.fori_loop(0, rows // tile, step, 0)

    for slab in range(heads // 2):
        parts = []
        for head in (2 * slab, 2 * slab + 1):
            got = total[head]
            weight = got[:, HEAD : HEAD + 1]
            parts.append(got / weight)
            ext[head] = with_minus(low[head].astype(F32), jnp.log(weight))
        joined = jnp.where(lane < HEAD, parts[0], pltpu.roll(parts[1], HEAD, 1))
        mixed[:, slab * LANES : (slab + 1) * LANES] = joined.astype(BF)
    block = rows // 4
    for i, at in enumerate(spots_of(spots, 4, rows)):
        moved[i * block : (i + 1) * block, :] = mixed[at, :]
    split_rows(nn_dot(moved[...], w_out[...]), *sums)


def attend_back_kernel(
    tile,
    count,
    seq,
    spots,
    seg,
    ext,
    mixed,
    own,
    near,
    far,
    far_near,
    w_out,
    q_raw,
    cosines,
    sines,
    gain_q,
    *refs,
):
    pieces = refs[:count]
    d_rows, furthest, d_q_raw, gain_part = refs[count : count + 4]
    d_pieces = (*refs[count + 4 : 2 * count + 3], furthest)
    d_ext, d_query, d_mixed = refs[2 * count + 3 :]
    rows = mixed.shape[0]
    heads = mixed.shape[1] // HEAD
    group = heads // 2
    me = spots[4]
    first_doc = spots[5 + seq]
    lane = lane_of((rows, LANES))
    block = rows // 4
    for i, part in enumerate((own, near, far, far_near)):
        d_rows[i * block : (i + 1) * block, :] = part[...]
    moved = nt_dot(d_rows[...], w_out[...]).astype(BF)
    for i, at in enumerate(spots_of(spots, 4, rows)):
        d_mixed[at, :] = moved[i * block : (i + 1) * block]
    for head in range(heads):
        grad = jnp.where(lane < HEAD, low_head(d_mixed, head), 0.0)
        delta = jnp.sum(grad * low_head(mixed, head), axis=-1, keepdims=True)
        d_ext[head] = with_minus(grad, delta)
    d_query[...] = jnp.zeros_like(d_query)
    low_tile = lane_of((tile, LANES)) < HEAD

    def tile_step(back, block, piece, d_piece):
        start = (me - back) * rows + block * tile
        needed = start + tile > first_doc
        at = pl.ds(block * tile, tile)

        @pl.when(needed)
        def _():
            kv = piece[at, :]
            shape = (tile, rows)
            place = start + lax.broadcasted_iota(jnp.int32, shape, 0)
            allowed = place >= seg[...]
            if back == 0:
                allowed &= place <= me * rows + lax.broadcasted_iota(jnp.int32, shape, 1)
            d_keys = []
            d_values = []
            for which in range(2):
                key_f = with_ones(kv[:, :LANES], which)
                key = key_f.astype(BF)
                key_t = key_f.T[:HEAD].astype(BF)
                value = with_ones(kv[:, LANES:], which).astype(BF)
                d_key = jnp.zeros((tile, LANES), F32)
                d_value = jnp.zeros((tile, LANES), F32)
                for head in range(which * group, (which + 1) * group):
                    scores = jnp.where(allowed, nt_dot(key, ext[head]), -1e30)
                    probs = jnp.exp(scores)
                    d_scores = (probs * nt_dot(value, d_ext[head])).astype(BF)
                    d_value += nn_dot(probs.astype(BF), d_ext[head])
                    d_key += nn_dot(d_scores, ext[head])
                    d_query[head * HEAD : (head + 1) * HEAD, :] += nn_dot(key_t, d_scores)
                d_keys.append(d_key)
                d_values.append(d_value)
            for spot, pair in enumerate((d_keys, d_values)):
                joined = jnp.where(low_tile, pair[0], pltpu.roll(pair[1], HEAD, 1))
                d_piece[at, spot * LANES : (spot + 1) * LANES] = joined.astype(BF)

        @pl.when(jnp.logical_not(needed))
        def _():
            d_piece[at, :] = jnp.zeros((tile, 2 * LANES), BF)

    for back, (piece, d_piece) in enumerate(zip(pieces, d_pieces)):

        @pl.when(me >= back)
        def _(back=back, piece=piece, d_piece=d_piece):
            def step(block, carry):
                tile_step(back, block, piece, d_piece)
                return carry

            lax.fori_loop(0, rows // tile, step, 0)

        @pl.when(me < back)
        def _(d_piece=d_piece):
            d_piece[...] = jnp.zeros_like(d_piece)

    for slab in range(heads // 2):
        at = slice(slab * LANES, (slab + 1) * LANES)
        grad = (d_query[at, :].T * 0.125).astype(BF).astype(F32)
        out, part = rope_norm_back(grad, q_raw[:, at], cosines[...], sines[...], gain_q[...])
        d_q_raw[:, at] = out
        gain_part[:, at] = part


def rope_norm_back(grad, raw, cosines, sines, gains):
    back = turn(grad, cosines, -sines)
    scale = lax.rsqrt(head_mean(raw * raw) + EPS)
    unit = raw * scale
    scaled = back * gains
    out = scale * (scaled - unit * head_mean(scaled * unit))
    part = jnp.sum(back * unit, axis=0, keepdims=True)
    return out.astype(BF), part


def key_back_kernel(
    quarters,
    d_piece,
    got,
    d_q_raw,
    k_raw,
    cosines,
    sines,
    gain_k,
    w_query,
    w_key,
    w_value,
    d_qkv,
    own,
    near,
    far,
    far_near,
    gain_part,
    moved,
):
    q_cols = d_q_raw.shape[1]
    total = (d_piece[...].astype(F32) + got[...].astype(F32)).astype(BF)
    d_key = total[:, :LANES].astype(F32)
    out, part = rope_norm_back(d_key, k_raw[...], cosines[...], sines[...], gain_k[...])
    gain_part[...] = part
    d_qkv[:, :q_cols] = d_q_raw[...]
    d_qkv[:, q_cols : q_cols + LANES] = out
    d_qkv[:, q_cols + LANES :] = total[:, LANES:]
    block = moved.shape[0] // 4
    for i, at in enumerate(spots_of(quarters, 4, moved.shape[0])):
        moved[i * block : (i + 1) * block, :] = d_qkv[at, :]
    grad = nt_dot(moved[:, :q_cols], w_query[...])
    grad += nt_dot(moved[:, q_cols : q_cols + LANES], w_key[...])
    grad += nt_dot(moved[:, q_cols + LANES :], w_value[...])
    split_rows(grad, own, near, far, far_near)


def keys_back_kernel(seqs, spots, *refs):
    pieces, d_queries, raws = (refs[i * seqs : (i + 1) * seqs] for i in range(3))
    got, *shared = refs[3 * seqs : 3 * seqs + 7]
    d_qkv, *outs, moved = refs[3 * seqs + 7 :]
    local = moved.shape[0]
    for s in range(seqs):
        at = pl.ds(s * local, local)
        key_back_kernel(
            spots,
            pieces[s],
            got.at[at],
            d_queries[s],
            raws[s],
            *shared,
            d_qkv.at[at],
            *outs[4 * s : 4 * s + 4],
            outs[4 * seqs + s],
            moved,
        )


def spots_of(spots, count, rows, skip=0):
    block = rows // count
    return [pl.ds(pl.multiple_of(spots[skip + i] * block, 16), block) for i in range(count)]


def split_rows(total, *parts):
    block = total.shape[0] // len(parts)
    for i, part in enumerate(parts):
        part[...] = total[i * block : (i + 1) * block].astype(part.dtype)


def d_active_kernel(quarters, rows, right, moved, out):
    @pl.when(pl.program_id(0) == 0)
    def _():
        block = rows.shape[0] // 4
        for i, at in enumerate(spots_of(quarters, 4, rows.shape[0])):
            moved[i * block : (i + 1) * block, :] = rows[at, :]

    out[...] = nt_dot(moved[...], right[...]).astype(BF)


def units_kernel(
    units, own, near, far, far_near, gate_t, up_t, d_active, rows, active, d_gate, d_upper
):
    @pl.when(pl.program_id(0) == 0)
    def _():
        block = own.shape[0]
        for i, part in enumerate((own, near, far, far_near)):
            rows[i * block : (i + 1) * block, :] = part[...]

    x = rows[...]
    wide = active.shape[1]
    half = wide // 2
    for part in range(2):
        at = slice(part * half, (part + 1) * half)
        gate = nt_dot(x, gate_t[at, :])
        upper = nt_dot(x, up_t[at, :])
        column = pl.program_id(0) * wide + part * half + lane_of(gate.shape)
        real = column < units
        sigma = jax.nn.sigmoid(gate)
        silu = gate * sigma
        grad = d_active[:, at].astype(F32)
        active[:, at] = jnp.where(real, silu * upper, 0.0).astype(BF)
        d_upper[:, at] = jnp.where(real, grad * silu, 0.0).astype(BF)
        slope = grad * upper * (sigma + silu * (1.0 - sigma))
        d_gate[:, at] = jnp.where(real, slope, 0.0).astype(BF)


def columns_kernel(count, *refs):
    depth = refs[count].shape[0]
    total = sum(nn_dot(refs[i][:, :depth], refs[count + i][...]) for i in range(count))
    split_rows(total, *refs[2 * count :])


def masked_sum(valid, values):
    mask = jnp.broadcast_to(valid[0].astype(F32), (8, values.shape[0]))
    high = values.astype(BF)
    low = (values - high.astype(F32)).astype(BF)
    mask = mask.astype(BF)
    return (nn_dot(mask, high) + nn_dot(mask, low))[:1]


def pass_back_kernel(first, second, *refs):
    out = refs[-1]
    local = first.shape[0]
    for i, part in enumerate((first, second)):
        at = slice(i * local, (i + 1) * local)
        if len(refs) > 1:
            out[at, :] = (part[...].astype(F32) + refs[0][at, :].astype(F32)).astype(BF)
        else:
            out[at, :] = part[...]


def norm_two_kernel(spot, kept, got_far, got, hidden, valid, gain, normed, middle, squares):
    attn = kept[...] + got_far[...].astype(F32) + got[...].astype(F32)
    before = hidden[...].astype(F32)
    total = before + attn
    middle[...] = total
    normed[...] = (total * rms_scale(total) * gain[...]).astype(BF)
    squares[0:1, :] = masked_sum(valid, attn * attn)
    squares[1:2, :] = masked_sum(valid, before * before)


def middle_back_kernel(spot, kept, got_far, got, middle, cot, gain, d_low, d_middle, gain_part):
    grad = kept[...] + got_far[...].astype(F32) + got[...].astype(F32)
    before = middle[...]
    scale = rms_scale(before)
    unit = before * scale
    gain_part[...] = jnp.sum(grad * unit, axis=0, keepdims=True)
    total = cot[...].astype(F32) + norm_back(grad, unit, scale, gain[...])
    d_middle[...] = total
    d_low[...] = total.astype(BF)


def hidden_back_kernel(spot, kept, got_far, got, hidden, d_middle, gain, out, gain_part):
    grad = kept[...] + got_far[...].astype(F32) + got[...].astype(F32)
    before = hidden[...].astype(F32)
    scale = rms_scale(before)
    unit = before * scale
    gain_part[...] = jnp.sum(grad * unit, axis=0, keepdims=True)
    out[...] = (d_middle[...] + norm_back(grad, unit, scale, gain[...])).astype(BF)


def output_kernel(spot, kept, got_far, got, middle, valid, out, squares):
    branch = kept[...] + got_far[...].astype(F32) + got[...].astype(F32)
    out[...] = (middle[...] + branch).astype(BF)
    squares[...] = masked_sum(valid, branch * branch)


def place_kernel(quarters, *refs):
    parts, out = refs[:-1], refs[-1]
    block = parts[0].shape[0]
    for i, part in enumerate(parts):
        first = pl.multiple_of((i // 4 * 4 + quarters[i % 4]) * block, 16)
        out[pl.ds(first, block), :] = part[...]


def rope_tables(length):
    places = np.arange(length).astype(np.float32)
    half = HEAD // 2
    freqs = np.float32(THETA) ** (-np.arange(half).astype(np.float32) / np.float32(half))
    angles = (places[:, None] * freqs.astype(np.float32)[None, :]).astype(np.float64)
    cosines = np.cos(angles).astype(np.float32)
    sines = np.sin(angles).astype(np.float32)
    return (
        np.concatenate([cosines] * 4, axis=1),
        np.concatenate([-sines, sines, -sines, sines], axis=1),
    )


def after(value, *others):
    return lax.optimization_barrier((value,) + others)[0]


def params():
    return pltpu.CompilerParams(vmem_limit_bytes=VMEM_LIMIT)


def call(kernel, name, **kw):
    small = pl.CostEstimate(flops=1, bytes_accessed=1, transcendentals=0)
    return pl.pallas_call(kernel, compiler_params=params(), cost_estimate=small, name=name, **kw)


def shape(*dims, dtype=BF):
    return jax.ShapeDtypeStruct(dims, dtype)


def fixed(*dims):
    return pl.BlockSpec(dims, lambda i: (0,) * len(dims))


def by_row(rows, cols, first=0):
    return pl.BlockSpec((rows, cols), lambda i: (first + i, 0))


def by_block(rows, cols, spot):
    return pl.BlockSpec((rows, cols), lambda i: (spot, 0))


def by_col(rows, cols):
    return pl.BlockSpec((rows, cols), lambda i: (0, i))


SMEM = pl.BlockSpec(memory_space=pltpu.SMEM)
UNITS = 512
WIDE_UNITS = 896
PAD = 256


def flip(n, bit):
    return [(i, i ^ bit) for i in range(n)]


def cut(array, start, size):
    return lax.dynamic_slice_in_dim(array, start, size, axis=0)


class Order:
    def __init__(self):
        self.last = None

    def tie(self, *values):
        if self.last is not None:
            values = lax.optimization_barrier(values + (self.last,))[:-1]
        return values

    def mark(self, value):
        self.last = value
        return value

    def wait(self, values, spot):
        values[spot] = self.mark(self.tie(values[spot])[0])


def build(mesh):
    dp_n, ctx_n, tp_n = (mesh.shape[a] for a in ("dp", "ctx", "tp"))
    blocks = dp_n * ctx_n

    def bits(axis, n):
        out = []
        while n > 1:
            n //= 2
            out.append((axis, n))
        return out

    steps = bits("dp", dp_n) + bits("ctx", ctx_n)[::-1]
    sizes = {"dp": dp_n, "ctx": ctx_n, "tp": tp_n}

    def swap(value, step):
        axis, bit = step
        return lax.ppermute(value, axis, flip(sizes[axis], bit))

    core, across = ("tp", 1), ("tp", 2)

    def bit_of(step):
        axis, bit = step
        return lax.axis_index(axis) // bit % 2

    def halves(part, step, outer):
        axis, bit = step
        left = 1 if axis == "dp" else outer * ctx_n // (2 * bit)
        view = part.reshape(left, 2, -1, part.shape[-1])
        mine = bit_of(step)
        pick = lambda which: lax.dynamic_index_in_dim(view, which, 1, keepdims=False).reshape(
            -1, part.shape[-1]
        )
        return pick(mine), pick(1 - mine)

    def body(
        hidden,
        cotangent,
        segments,
        valid,
        w_query,
        w_key,
        w_value,
        w_out,
        w_gate,
        w_up,
        w_down,
        gain_attn,
        gain_ffn,
        gain_query,
        gain_key,
    ):
        seqs, local, width = hidden.shape
        rows = seqs * local
        every = range(seqs)
        q_cols = w_query.shape[1]
        units = w_gate.shape[1]
        wide = pl.cdiv(units, PAD) * PAD
        heads = q_cols // HEAD
        me = lax.axis_index("ctx")
        member = lax.axis_index("tp")
        o = Order()
        cosines, sines = (jnp.asarray(t) for t in rope_tables(local * ctx_n))
        hidden_r = hidden.reshape(rows, width)
        cot_r = cotangent.reshape(rows, width)
        valid_r = valid.reshape(seqs * 4, 1, local // 4)
        gate_t, up_t = w_gate.T, w_up.T
        gq = jnp.concatenate([gain_query, gain_query])[None]
        gk = jnp.concatenate([gain_key, gain_key])[None]
        gain_a, gain_f = gain_attn[None], gain_ffn[None]
        tile = 256
        half, quarter = local // 2, local // 4
        own = (member % 2) * 2 + member // 2
        spots = jnp.stack([own ^ i for i in range(4)] + [me])
        spots = jnp.concatenate([spots, segments[:, 0]]).astype(jnp.int32)
        seg_rows = [segments[s][None] for s in every]
        _, *seg_rows = lax.optimization_barrier((spots, *seg_rows))

        def stage(kernel, name, args, outs, grid=1, scratch=(), placed=False, shared=None):
            arrays = [a for a, _ in args]
            arrays[:1] = o.tie(arrays[0])
            fix = lambda spec: pl.BlockSpec(spec.block_shape, lambda i, *s: spec.index_map(i))
            of = lambda spec: spec.spec if isinstance(spec, Dynamic) else fix(spec)
            specs = [of(spec) for _, spec in args]
            old = list(shared or [])
            count = int(placed) + len(args)
            run = kernel
            if old:
                run = lambda *refs: kernel(*refs[:count], *refs[count + len(old) :])
            got = pl.pallas_call(
                run,
                grid_spec=pltpu.PrefetchScalarGridSpec(
                    num_scalar_prefetch=int(placed),
                    grid=(grid,),
                    in_specs=specs + [pl.BlockSpec(memory_space=pl.ANY)] * len(old),
                    out_specs=[fix(s) for _, s in outs],
                    scratch_shapes=list(scratch),
                ),
                out_shape=[s for s, _ in outs],
                input_output_aliases={count + i: i for i in range(len(old))},
                compiler_params=params(),
                cost_estimate=pl.CostEstimate(flops=1, bytes_accessed=1, transcendentals=0),
                name=name,
            )(*([spots] if placed else []), *arrays, *old)
            o.mark(got[0])
            return got

        class Dynamic:
            def __init__(self, cols, seq):
                self.spec = pl.BlockSpec((quarter, cols), lambda i, s: (seq * 4 + s[0], 0))

        def full(array):
            return (array, fixed(*array.shape))

        def fulls(arrays):
            return [full(a) for a in arrays]

        def new(*dims, dtype=BF):
            return (shape(*dims, dtype=dtype), fixed(*dims))

        def part(cols, s):
            return by_block(local, cols, s)

        class Table(Dynamic):
            def __init__(self, rows):
                per = local // rows
                self.spec = pl.BlockSpec((rows, LANES), lambda i, s: (s[4] * per + i, 0))

        class Valid(Dynamic):
            def __init__(self, seq):
                self.spec = pl.BlockSpec((1, 1, quarter), lambda i, s: (seq * 4 + s[0], 0, 0))

        tables = lambda n: [(t, Table(n)) for t in (cosines, sines)]

        parts_out = [
            (shape(quarter, width, dtype=d), fixed(quarter, width)) for d in (F32, F32, BF, BF)
        ]

        def split_columns(which, lefts, rights, name):
            count = len(lefts)
            depth, cols = rights[0].shape
            tokens = local * len(which)
            outs = stage(
                functools.partial(columns_kernel, count),
                name,
                [(l, by_block(tokens, l.shape[1], which[0] // len(which))) for l in lefts]
                + [(r, by_col(depth, UNITS)) for r in rights],
                [(out, by_col(quarter, UNITS)) for out, _ in parts_out] * len(which),
                grid=cols // UNITS,
            )
            return [outs[i * 4 : i * 4 + 4] for i in range(len(which))]

        class Spread:
            def __init__(self, own, near, far, far_near):
                self.own, self.near = own, near
                self.far = [far_near, far]

            def first(self):
                self.far = list(o.tie(*self.far))
                o.mark(self.far[0])
                self.got = [swap(f, core) for f in self.far]

            def second(self):
                near, got = o.tie(self.near, self.got[0])
                away = o.mark((near + got.astype(F32)).astype(BF))
                self.got[0] = swap(away, across)

            def parts(self):
                return fulls([self.own, self.got[1], self.got[0]])

        class Collect:
            def __init__(self, mine):
                self.got = [mine, swap(mine, across)]

            def second(self):
                o.wait(self.got, 1)
                self.got += [swap(value, core) for value in self.got]

        half_of = lambda left, which: lax.dynamic_slice_in_dim(
            left, which * (width // 2), width // 2, axis=1
        )

        def other_ctx(left, which):
            view = left.reshape(rows, blocks // 2, 2, width // blocks)
            return lax.dynamic_index_in_dim(view, which, 2, keepdims=False).reshape(rows, -1)

        class Grad:
            def __init__(self, *pairs, ctx_first=False):
                dp_bits = [step for step in steps if step[0] == "dp"]
                ctx_bits = [step for step in steps if step[0] == "ctx"]
                self.steps = ctx_bits + dp_bits if ctx_first else dp_bits + ctx_bits
                self.outer = dp_n if ctx_first else 1
                pick = other_ctx if ctx_first else half_of
                bit = bit_of(self.steps[0])
                self.rights = [right for _, right in pairs]
                self.keep = [lambda left=left: pick(left, bit) for left, _ in pairs]
                self.give = [lambda left=left: pick(left, 1 - bit) for left, _ in pairs]

            def away(self):
                rights = o.tie(*self.rights)
                parts = [tn_dot(left(), r).astype(BF) for left, r in zip(self.give, rights)]
                self.out = o.mark(jnp.concatenate(parts, axis=1))

            def send(self, *waits):
                for grad in waits:
                    grad.wait()
                (out,) = o.tie(self.out)
                self.got = swap(o.mark(out), self.steps[0])
                self.left_steps = self.steps[1:]

            def wait(self):
                (self.got,) = o.tie(self.got)
                o.mark(self.got)

            def columns(self, got):
                ends = np.cumsum([r.shape[1] for r in self.rights])
                return [got[:, e - r.shape[1] : e] for r, e in zip(self.rights, ends)]

            def own(self):
                *rights, got = o.tie(*self.rights, self.got)
                self.terms = []
                for left, r, g in zip(self.keep, rights, self.columns(got)):
                    self.terms.append([o.mark(tn_dot(left(), r) + g.astype(F32))])
                self.pass_on()

            def pass_on(self):
                if not self.left_steps:
                    return
                step = self.left_steps.pop(0)
                stay, away = [], []
                for terms in self.terms:
                    pairs = [halves(t, step, self.outer) for t in terms]
                    stay.append([p[0] for p in pairs])
                    away.append(sum(p[1].astype(F32) for p in pairs).astype(BF))
                got = swap(o.mark(jnp.concatenate(away, axis=1)), step)
                self.terms = [t + [g] for t, g in zip(stay, self.columns(got))]

            def arrive(self):
                for terms in self.terms:
                    (terms[-1],) = o.tie(terms[-1])

            def third(self):
                self.arrive()
                self.pass_on()

            def last(self):
                while self.left_steps:
                    self.third()
                self.arrive()
                return [o.mark(sum(t.astype(F32) for t in terms)) for terms in self.terms]

        up = lambda hops: [(i, i + hops) for i in range(ctx_n - hops)]
        down = [(i + 1, i) for i in range(ctx_n - 1)]
        normed, k_raw, pieces = None, [], []
        step = 256
        per = local // step

        class Around(Dynamic):
            def __init__(self):
                self.spec = pl.BlockSpec((step, LANES), lambda i, s: (s[4] * per + i % per, 0))

        for s in every:
            normed, sent, raw = stage(
                key_value_kernel,
                "key_value",
                [(hidden_r, by_row(step, width, s * per))]
                + fulls([gain_a, w_key, w_value])
                + tables(step)
                + fulls([gk]),
                [
                    (shape(rows, width), by_row(step, width, s * per)),
                    (shape(local, 2 * LANES), by_row(step, 2 * LANES)),
                    (shape(local, LANES, dtype=F32), by_row(step, LANES)),
                ],
                grid=per,
                placed=True,
                shared=[normed] if s else None,
            )
            k_raw.append(raw)
            pieces.append([sent])

        def send_keys(s, direct):
            for hops in range(1, ctx_n if direct else min(3, ctx_n)):
                pieces[s].append(lax.ppermute(pieces[s][0], "ctx", up(hops)))

        for s in every:
            send_keys(s, True)
        query, q_raw = stage(
            query_kernel,
            "query",
            [(normed, by_row(step, width)), full(w_query)]
            + [(t, Around()) for t in (cosines, sines)]
            + fulls([gq]),
            [(shape(rows, q_cols, dtype=d), by_row(step, q_cols)) for d in (BF, F32)],
            grid=seqs * per,
            placed=True,
        )
        d_active, cot_moved = [], None

        def d_active_of(s):
            nonlocal cot_moved
            cot_moved, grad = stage(
                d_active_kernel,
                "d_active",
                [(cot_r, part(width, s)), (w_down, by_row(WIDE_UNITS, width))],
                [
                    (shape(rows, width), part(width, s)),
                    (shape(local, wide), by_col(local, WIDE_UNITS)),
                ],
                grid=pl.cdiv(wide, WIDE_UNITS),
                placed=True,
                shared=[cot_moved] if s else None,
            )
            d_active.append(grad)

        d_active_of(0)
        for s in every[1:]:
            d_active_of(s)

        mixed, mixed_moved, exts, attn = [], None, [], []

        def attend(s):
            nonlocal mixed_moved
            mixed_moved, *parts, mix, ext = stage(
                functools.partial(attend_kernel, tile, s),
                "attend",
                [full(seg_rows[s]), (query, part(q_cols, s))] + fulls([w_out] + pieces[s]),
                [(shape(rows, q_cols), part(q_cols, s))]
                + parts_out
                + [new(local, q_cols), new(heads, local, LANES)],
                scratch=[
                    pltpu.VMEM((heads, local, LANES), BF),
                    pltpu.VMEM((heads, local, LANES), F32),
                    pltpu.VMEM((local, 1), jnp.int32),
                ],
                placed=True,
                shared=[mixed_moved] if s else None,
            )
            mixed.append(mix)
            exts.append(ext)
            attn.append(Spread(*parts))

        middle, squares, two = [], [], []

        def norm_two(s):
            normed_own, mid, square = stage(
                norm_two_kernel,
                "norm_two",
                attn[s].parts()
                + [(hidden_r, Dynamic(width, s)), (valid_r, Valid(s)), full(gain_f)],
                [new(quarter, width), new(quarter, width, dtype=F32), new(2, width, dtype=F32)],
                placed=True,
            )
            middle.append(mid)
            squares.append(square)
            two.append(Collect(normed_own))

        two_rows = active = d_gate = d_upper = None

        def units_of(s):
            nonlocal two_rows, active, d_gate, d_upper
            outs = (two_rows, active, d_gate, d_upper)
            two_rows, active, d_gate, d_upper = stage(
                functools.partial(units_kernel, units),
                "units",
                fulls(two[s].got)
                + [(gate_t, by_row(UNITS, width)), (up_t, by_row(UNITS, width))]
                + [(d_active[s], by_col(local, UNITS))],
                [(shape(rows, width), part(width, s))]
                + [(shape(rows, wide), pl.BlockSpec((local, UNITS), lambda i: (s, i)))] * 3,
                grid=pl.cdiv(wide, UNITS),
                shared=outs if s else None,
            )

        for s in every:
            attend(s)
        for s in every:
            attn[s].first()
        for s in every:
            attn[s].second()
        for s in every:
            norm_two(s)
        for s in every:
            two[s].second()
            units_of(s)

        down_sum = Grad((cot_moved, active))
        gate_sum = Grad((two_rows, d_gate))
        up_sum = Grad((two_rows, d_upper))
        down_sum.away()
        down_sum.send()
        d_two = [
            Spread(*parts)
            for parts in split_columns(every, [d_gate, d_upper], [gate_t, up_t], "d_two")
        ]
        for s in every:
            d_two[s].first()
        for s in every:
            d_two[s].second()

        branch, out_squares, out_parts = [], [], []

        def branch_of(s):
            branch.append(Spread(*split_columns([s], [active], [w_down], "branch")[0]))

        def output_of(s):
            value, square = stage(
                output_kernel,
                "output",
                branch[s].parts() + [full(middle[s]), (valid_r, Valid(s))],
                [new(quarter, width), new(1, width, dtype=F32)],
                placed=True,
            )
            out_squares.append(square)
            out_parts.append(Collect(value))

        d_middle, d_low, gain_f_parts = [], [], []

        def middle_back(s):
            low, mid, gains = stage(
                middle_back_kernel,
                "middle_back",
                d_two[s].parts() + [full(middle[s]), (cot_r, Dynamic(width, s)), full(gain_f)],
                [new(quarter, width), new(quarter, width, dtype=F32), new(1, width, dtype=F32)],
                placed=True,
            )
            d_middle.append(mid)
            gain_f_parts.append(gains)
            d_low.append(Collect(low))

        branch_of(0)
        for s in every:
            middle_back(s)
        for s in every[1:]:
            branch_of(s)
        d_low[0].second()
        gate_sum.away()
        down_sum.wait()
        up_sum.away()
        gate_sum.send()
        down_sum.own()
        for s in every[1:]:
            d_low[s].second()
        for s in every:
            branch[s].first()

        d_q_raw, d_pieces, d_rows, passed = [], [], None, None
        gain_q_parts = []

        def attend_back(s):
            nonlocal d_rows, passed
            outs = stage(
                functools.partial(attend_back_kernel, tile, ctx_n, s),
                "attend_back",
                fulls([seg_rows[s], exts[s], mixed[s]] + d_low[s].got + [w_out])
                + [(q_raw, part(q_cols, s))]
                + tables(local)
                + fulls([gq] + pieces[s]),
                [
                    (shape(rows, width), part(width, s)),
                    (shape(rows, 2 * LANES), part(2 * LANES, s)),
                    new(local, q_cols),
                    new(1, q_cols, dtype=F32),
                ]
                + [new(local, 2 * LANES)] * (ctx_n - 1),
                scratch=[
                    pltpu.VMEM((heads, local, LANES), BF),
                    pltpu.VMEM((q_cols, local), F32),
                    pltpu.VMEM((local, q_cols), BF),
                ],
                placed=True,
                shared=[d_rows, passed] if s else None,
            )
            d_rows, passed = outs[:2]
            d_q_raw.append(outs[2])
            gain_q_parts.append(outs[3])
            d_pieces.append(outs[4:])

        def pass_back(back):
            nonlocal passed
            if back < ctx_n - 1:
                args = fulls([d_pieces[s][back] for s in every] + [passed])
                passed = stage(pass_back_kernel, "pass_back", args, [new(rows, 2 * LANES)])[0]
            passed = lax.ppermute(passed, "ctx", down)

        d_qkv, d_one, gain_k_parts = None, [], []

        def key_back():
            nonlocal d_qkv
            wide_out = q_cols + 2 * LANES
            d_qkv, *outs = stage(
                functools.partial(keys_back_kernel, seqs),
                "key_back",
                fulls([d_pieces[s][0] for s in every] + d_q_raw + k_raw + [passed])
                + tables(local)
                + fulls([gk, w_query, w_key, w_value]),
                [new(rows, wide_out)] + parts_out * seqs + [new(1, LANES, dtype=F32)] * seqs,
                scratch=[pltpu.VMEM((local, wide_out), BF)],
                placed=True,
            )
            for s in every:
                d_one.append(Spread(*outs[4 * s : 4 * s + 4]))
                gain_k_parts.append(outs[4 * seqs + s])

        gain_a_parts, back_hidden = [], []

        def hidden_back(s):
            grad, gains = stage(
                hidden_back_kernel,
                "hidden_back",
                d_one[s].parts()
                + [(hidden_r, Dynamic(width, s)), full(d_middle[s]), full(gain_a)],
                [new(quarter, width), new(1, width, dtype=F32)],
                placed=True,
            )
            gain_a_parts.append(gains)
            back_hidden.append(Collect(grad))

        def place(parts):
            return stage(
                place_kernel,
                "place",
                fulls([p for c in parts for p in c.got]),
                [new(rows, width)],
                placed=True,
            )[0]

        attend_back(0)
        for s in every:
            branch[s].second()
        down_sum.third()
        for s in every[1:]:
            attend_back(s)
        up_sum.send(gate_sum)
        if ctx_n > 1:
            pass_back(ctx_n - 1)
        (grad_down,) = down_sum.last()
        for i, back in enumerate(range(ctx_n - 2, 0, -1)):
            pass_back(back)
            if i == 0:
                for s in every:
                    output_of(s)
        gate_sum.own()
        for s in every:
            out_parts[s].second()
        key_back()
        for s in every:
            d_one[s].first()
        rest_sum = Grad((normed, d_qkv), (d_rows, mixed_moved))
        rest_sum.away()
        rest_sum.send(up_sum)
        for s in every:
            d_one[s].second()
        up_sum.own()
        gate_sum.third()
        output = place(out_parts).reshape(seqs, local, width)
        for s in every:
            hidden_back(s)
        rest_sum.wait()
        rest_sum.own()
        for s in every:
            back_hidden[s].second()
        (grad_gate,) = gate_sum.last()

        gain_q_part = sum(gain_q_parts).reshape(heads, HEAD).sum(axis=0)
        gain_k_part = sum(gain_k_parts).reshape(2, HEAD).sum(axis=0)
        total_square = sum(squares).sum(axis=1)
        branch_square = sum(out_squares).sum()
        count = jnp.sum(valid).astype(F32) / tp_n
        small = jnp.concatenate(
            [
                sum(gain_a_parts)[0],
                sum(gain_f_parts)[0],
                gain_q_part,
                gain_k_part,
                jnp.stack([total_square[1], total_square[0], branch_square, count]),
                jnp.zeros((LANES - 4,), F32),
            ]
        ).reshape(-1, LANES)
        (small,) = o.tie(small)
        flips = [(a, b) for a in ("tp", "dp", "ctx") for _, b in bits(a, sizes[a])[::-1]]

        def sum_step():
            nonlocal small
            small, got = o.tie(small, swap(small, flips.pop(0)))
            small = o.mark(small + got)

        ctx_flips = sum(1 for axis, _ in flips if axis == "ctx")
        while len(flips) > ctx_flips:
            sum_step()
        up_sum.third()
        grad_hidden = place(back_hidden).reshape(seqs, local, width)
        while len(flips) > 1:
            sum_step()
        rest_sum.third()
        (grad_up,) = up_sum.last()
        while flips:
            sum_step()
        grad_qkv, grad_out = rest_sum.last()
        grad_down, grad_gate, grad_up = (g[:, :units] for g in (grad_down, grad_gate, grad_up))
        grad_down, grad_out = grad_down.T, grad_out.T

        small = small.reshape(-1)
        at = 2 * width + 2 * HEAD
        denom = jnp.maximum(small[at + 3], 1.0) * width
        root = lambda spot: jnp.sqrt(small[at + spot] / denom)
        return (
            output,
            grad_hidden,
            grad_qkv[:, :q_cols],
            grad_qkv[:, q_cols : q_cols + LANES],
            grad_qkv[:, q_cols + LANES :],
            grad_out,
            grad_gate,
            grad_up,
            grad_down,
            small[:width],
            small[width : 2 * width],
            small[2 * width : 2 * width + HEAD],
            small[2 * width + HEAD : at],
            root(0),
            root(1),
            root(2),
        )

    return body


def solution(mesh):
    tokens = P("dp", "ctx", None)
    marks = P("dp", "ctx")
    columns = P(None, "tp")
    rows = P("tp", None)
    by_rows = P(("dp", "ctx"), "tp")
    by_columns = P("tp", ("dp", "ctx"))
    in_specs = (tokens, tokens, marks, marks, columns, columns, columns, rows)
    in_specs += (columns, columns, rows, P(), P(), P(), P())
    out_specs = (tokens, tokens, by_rows, by_rows, by_rows, by_columns, by_rows, by_rows)
    out_specs += (by_columns, P(), P(), P(), P(), P(), P(), P())
    return jax.shard_map(
        build(mesh), mesh=mesh, in_specs=in_specs, out_specs=out_specs, check_vma=False
    )
```
